128 devices in a mesh: row: 8 (over x, core), col: 16 (over y, z).
Axes of the slice: x: 4, y: 4, z: 4, core: 2. Of those that a mesh axis runs over, the one named last changes fastest.
Arguments:
- features: bfloat16 [131072, 128], P(('row', 'col')), may hold values from -6 to 6
- weight: bfloat16 [128, 128], replicated, may hold values from -0.5 to 0.5
- bias_vector: float32 [128], replicated, may hold values from -3 to 3
- stripe_values: bfloat16 [131072, 8192], P(('row', 'col')), may hold values from -0.0625 to 0.0625
- tile_values: bfloat16 [4096, 128, 128], P(('row', 'col')), may hold values from -0.25 to 0.25
- tile_rows: int32 [4096], P(('row', 'col')), may hold values from 0 to 7
- tile_slots: int32 [4096], P(('row', 'col')), may hold values from 0 to 15
- send_lists: int32 [8, 16, 16, 1], P('row', 'col'), may hold values from 0 to 7
- cotangent: bfloat16 [131072, 128], P(('row', 'col')), may hold values from -6 to 6
Outputs:
- hidden_out: bfloat16 [131072, 128], P(('row', 'col'))
- grad_features: bfloat16 [131072, 128], P(('row', 'col'))
- grad_weight: float32 [128, 128], replicated
- grad_bias: float32 [128], replicated
The draws below stay inside these ranges and needn't reach their ends.
All inputs are finite; a program needn't handle non-finite values.
Results may differ from the reference program's by a relative error of at most 0.02.
Values may be sent and summed in bfloat16 or wider, within the bound.
A program may use at most 128 MiB of HBM per device.

```python
import math
import jax
import jax.numpy as jnp
from jax import lax

F = 128
BLK = 128
NODE_DEV = 1024
S = 1
NT = 32
BLOCKS_DEV = 8
NODES = 131072
TILES = 4096
STRIPE = 8192
N_ROW = 8
N_COL = 16


def place_ends(drawn, rng, low, largest):
    shape = drawn.shape
    spot = [jax.random.randint(jax.random.fold_in(rng, axis), (), 0, shape[axis]) for axis in range(len(shape))]
    drawn = drawn.at[tuple(spot)].set(low)
    longest = shape.index(max(shape))
    spot[longest] = (spot[longest] + 1) % shape[longest]
    return drawn.at[tuple(spot)].set(largest)


def levels(rng, shape, cuts, low, top_value):
    level = 1.0
    for position, blocks in cuts:
        heights = jax.random.uniform(jax.random.fold_in(jax.random.fold_in(rng, 6), position), (blocks,), jnp.float32, low / len(cuts), top_value / len(cuts))
        level = level * jnp.repeat(jnp.exp(heights), shape[position] // blocks).reshape((-1,) + (1,) * (len(shape) - 1 - position))
    return level


def centred(stream_key, shape, width, limit, cuts=(), kind=jnp.bfloat16):
    drawn = jax.random.normal(stream_key, shape, jnp.float32) * width
    if len(cuts) > 0:
        drawn = levels(stream_key, shape, cuts, -0.22, 0.18) * drawn
    return jnp.clip(drawn, min=-limit, max=limit).astype(kind)


def setup_inputs(seed: int = 0) -> dict:
    arg_keys = jax.random.split(jax.random.key(seed), 10)
    features = centred(arg_keys[0], (NODES, F), 1.0, 6.0, ((0, 128),))
    weight = centred(arg_keys[1], (F, F), F ** -0.5, 0.5)
    bias_vector = centred(arg_keys[2], (F,), 0.5, 3.0, (), jnp.float32)
    stripe_values = centred(arg_keys[3], (NODES, STRIPE), (N_ROW * NODE_DEV) ** -0.5, 0.0625, ((0, 128),))
    tile_values = centred(arg_keys[4], (TILES, BLK, BLK), (BLK * NT // BLOCKS_DEV) ** -0.5, 0.25, ((0, 128),))
    tile_rows = place_ends(jax.random.randint(arg_keys[5], (TILES,), 0, BLOCKS_DEV), jax.random.fold_in(arg_keys[5], 1), 0, BLOCKS_DEV - 1).astype(jnp.int32)
    tile_slots = place_ends(jax.random.randint(arg_keys[6], (TILES,), 0, N_COL * S), jax.random.fold_in(arg_keys[6], 1), 0, (N_COL * S) - 1).astype(jnp.int32)
    send_lists = place_ends(jax.random.randint(arg_keys[7], (N_ROW, N_COL, N_COL, S), 0, BLOCKS_DEV), jax.random.fold_in(arg_keys[7], 1), 0, BLOCKS_DEV - 1).astype(jnp.int32)
    cotangent = centred(arg_keys[8], (NODES, F), 1.0, 6.0, ((0, 128),))
    return dict(features=features, weight=weight, bias_vector=bias_vector, stripe_values=stripe_values, tile_values=tile_values, tile_rows=tile_rows, tile_slots=tile_slots, send_lists=send_lists, cotangent=cotangent)


def reference(features, weight, bias_vector, stripe_values, tile_values, tile_rows, tile_slots, send_lists, cotangent):
    devices_all = N_ROW * N_COL
    blocks_here = NODE_DEV // BLK
    projected = jnp.dot(features, weight, preferred_element_type=jnp.float32).astype(jnp.bfloat16)
    sources = jnp.transpose(projected.reshape(N_ROW, N_COL, NODE_DEV, F), (1, 0, 2, 3)).reshape(N_COL, N_ROW * NODE_DEV, F)
    stripe_three = stripe_values.reshape(devices_all, NODE_DEV, N_ROW * NODE_DEV)
    device_list = jnp.arange(devices_all, dtype=jnp.int32)

    def stripe_forward(device):
        return jnp.dot(stripe_three[device], sources[device % N_COL], preferred_element_type=jnp.float32)
    dense_sum = lax.map(stripe_forward, device_list)
    tiles = tile_values.reshape(devices_all, NT, BLK, BLK).astype(jnp.float32)
    rows_of = tile_rows.reshape(devices_all, NT)
    slots_of = tile_slots.reshape(devices_all, NT)
    device_ids = device_list[:, None]
    row_ids = device_ids // N_COL
    col_ids = device_ids % N_COL
    peer_ids = slots_of // S
    place_ids = slots_of % S
    source_block = send_lists[row_ids, peer_ids, col_ids, place_ids]
    source_device = row_ids * N_COL + peer_ids
    projected_blocks = projected.reshape(devices_all, blocks_here, BLK, F)
    gathered = projected_blocks[source_device, source_block].astype(jnp.float32)
    products = jnp.einsum('dtij,dtjf->dtif', tiles, gathered)
    sparse_sum = jnp.zeros((devices_all, blocks_here, BLK, F), jnp.float32).at[device_ids, rows_of].add(products)
    total = dense_sum.reshape(NODES, F) + sparse_sum.reshape(NODES, F)
    shifted = total + bias_vector.astype(jnp.float32)
    sigmoid_part = jax.nn.sigmoid(shifted)
    hidden_out = (shifted * sigmoid_part).astype(jnp.bfloat16)
    slope = sigmoid_part * (1.0 + shifted * (1.0 - sigmoid_part))
    grad_pre = (cotangent.astype(jnp.float32) * slope).astype(jnp.bfloat16)
    grad_rows = grad_pre.reshape(devices_all, NODE_DEV, F)

    def stripe_backward(device):
        return lax.dot_general(stripe_three[device], grad_rows[device], (((0,), (0,)), ((), ())), preferred_element_type=jnp.float32)
    dense_back = lax.map(stripe_backward, device_list)
    dense_back = dense_back.reshape(N_ROW, N_COL, N_ROW, NODE_DEV, F).sum(axis=0)
    dense_back = jnp.transpose(dense_back, (1, 0, 2, 3)).reshape(NODES, F)
    row_grads = grad_pre.reshape(devices_all, blocks_here, BLK, F)[device_ids, rows_of].astype(jnp.float32)
    back_products = jnp.einsum('dtji,dtjf->dtif', tiles, row_grads)
    sparse_back = jnp.zeros((devices_all, blocks_here, BLK, F), jnp.float32).at[source_device, source_block].add(back_products)
    grad_proj = (dense_back + sparse_back.reshape(NODES, F)).astype(jnp.bfloat16)
    grad_features = lax.dot_general(grad_proj, weight, (((1,), (1,)), ((), ())), preferred_element_type=jnp.float32).astype(jnp.bfloat16)
    scale = 1.0 / math.sqrt(NODES)
    grad_weight = lax.dot_general(features, grad_proj, (((0,), (0,)), ((), ())), preferred_element_type=jnp.float32) * scale
    grad_bias = lax.optimization_barrier(jnp.sum(grad_pre.astype(jnp.float32), axis=0)) * scale
    return (hidden_out, grad_features, grad_weight, grad_bias)
```

```python
import functools
import math

import jax
import jax.numpy as jnp
from jax import lax
from jax.experimental import pallas as pl
from jax.experimental.pallas import tpu as pltpu
from jax.sharding import PartitionSpec as P

MESH = pl.DeviceIdType.MESH
BF16 = jnp.bfloat16
F32 = jnp.float32
AG = 4
RS = 4


def mm(a, b):
    return jnp.dot(a, b, preferred_element_type=F32)


def order(read, n, lanes=128):
    sub = lax.broadcasted_iota(jnp.int32, (n, lanes), 0)
    lane = lax.broadcasted_iota(jnp.int32, (n, lanes), 1)
    col = jnp.zeros((n, lanes), jnp.int32)
    row = jnp.full((n, lanes), 1 << 20, jnp.int32)

    def one(t, both):
        v = read(t)
        return jnp.where(sub == t, v, both[0]), jnp.where(lane == t, v * n + t, both[1])

    col, row = lax.fori_loop(0, n, one, (col, row))
    less = (row < col * n + sub).astype(jnp.int32)
    rank = jnp.sum(less, axis=1, keepdims=True)
    hit = rank == lane
    perm = jnp.sum(jnp.where(hit, sub, 0), axis=0, keepdims=True)
    value = jnp.sum(jnp.where(hit, col, 0), axis=0, keepdims=True)
    last = jnp.sum((col <= lane).astype(jnp.int32), axis=0, keepdims=True)
    count = jnp.sum((col == lane).astype(jnp.int32), axis=0, keepdims=True)
    last = jnp.where(count > 0, last, 0)
    before = jnp.sum(((row // n == col) & (lane < sub)).astype(jnp.int32), axis=1, keepdims=True)
    again = jnp.sum(jnp.where(hit & (before > 0), 1, 0), axis=0, keepdims=True)
    return jnp.concatenate([perm, value, last, again] + [jnp.zeros_like(perm)] * 4, axis=0)


def kernel(
    nrow, ncol, scale,
    feat, weight, bias, stripe, tiles, rows_s, slots_s, lists_s, cot,
    hid_out, gf_out, gw_out, gb_out,
    st, fo, fg, tv, cv, recv, stage, meta_v, meta_s, scan, y, yb, gp, hid, gt, gtb,
    pa, ps, sr, xs, ra, rb, bst, brecv, gws, gwr, g2s, g2r, gwo, gfv, biasp,
    lsem, ssem, rsem, fsem, frsem, bsem, brsem, a1s, a1r, a2s, a2r, a3s, a3r,
):
    nblk, blk, _ = feat.shape
    nt = tv.shape[0]
    nodes = nblk * blk
    r = lax.axis_index("row")
    c = lax.axis_index("col")
    chip, core = r // 2, r % 2
    chips = nrow // 2
    chip_r, chip_l, chip_f = (chip + 1) % chips, (chip + chips - 1) % chips, (chip + 2) % chips
    sib = chip * 2 + 1 - core
    right, left = chip_r * 2 + core, chip_l * 2 + core
    order_of = [
        chip * 2 + core, chip * 2 + 1 - core,
        chip_l * 2 + core, chip_l * 2 + 1 - core,
        chip_r * 2 + core, chip_r * 2 + 1 - core,
        chip_f * 2 + core, chip_f * 2 + 1 - core,
    ]

    def peer(d):
        return lax.rem(c + d, ncol)

    local = [
        pltpu.make_async_copy(feat, fo, lsem.at[8]),
        pltpu.make_async_copy(cot, cv, lsem.at[9]),
        pltpu.make_async_copy(tiles, tv, lsem.at[10]),
    ]
    local[0].start()
    stripes = [
        pltpu.make_async_copy(
            stripe.at[:, pl.ds(pl.multiple_of(order_of[k] * nodes, 128), nodes)], st.at[k], lsem.at[k]
        )
        for k in range(8)
    ]
    stripes[0].start()
    stripes[1].start()
    local[2].start()
    for k in range(2, 8):
        stripes[k].start()
    local[1].start()

    barrier = pltpu.get_barrier_semaphore()

    def greet_col(d, _):
        pl.semaphore_signal(barrier, inc=1, device_id=(r, peer(d)), device_id_type=MESH)
        return 0

    def greet_row(d, _):
        pl.semaphore_signal(barrier, inc=1, device_id=(lax.rem(r + d, nrow), c), device_id_type=MESH)
        return 0

    lax.fori_loop(1, nrow, greet_row, 0)
    lax.fori_loop(1, ncol, greet_col, 0)

    meta_v[0:8] = order(lambda t: rows_s[t], nt)
    meta_v[8:16] = order(lambda t: lax.rem(c + ncol - slots_s[t], ncol), nt)
    meta_v[16:24] = order(lambda d: lists_s[peer(d)], ncol)
    meta_copy = pltpu.make_async_copy(meta_v, meta_s, lsem.at[11])
    meta_copy.start()

    pl.semaphore_wait(barrier, nrow - 1 + ncol - 1)

    piece, half = nodes // AG, AG // 2
    pb = piece // blk
    width, rhalf = nodes // RS, RS // 2

    def remote(i, src, dst, row):
        return pltpu.make_async_remote_copy(
            src_ref=src, dst_ref=dst, send_sem=ssem.at[i], recv_sem=rsem.at[i],
            device_id=(row, c), device_id_type=MESH,
        )

    def part(slot, p):
        own = fo if slot == 0 else fg.at[slot - 1]
        return own.at[pl.ds(p * pb, pb)]

    def own_right(p):
        return remote(p, part(0, p), part(2, p), right)

    def own_left(p):
        return remote(AG + p, part(0, p), part(4, p), left)

    def on_right(p):
        return remote(2 * AG + p, part(2, p), part(6, p), right)

    def on_left(p):
        return remote(2 * AG + p, part(4, p), part(6, p), left)

    def to_twin(slot, p):
        return remote(3 * AG + (slot - 2) // 2 * AG + p, part(slot, p), part(slot + 1, p), sib)

    own_twin = remote(6 * AG, fo, fg.at[0], sib)
    base = 6 * AG + 1

    def give(q, p):
        return remote(base + q * RS + p, ps.at[q, p], sr.at[q, p], sib)

    def first_right(p):
        return remote(base + 4 * RS + p, xs.at[2, p], ra.at[p], right)

    def first_left(p):
        return remote(base + 4 * RS + p, xs.at[2, p], ra.at[p], left)

    def last_right(p):
        return remote(base + 5 * RS + p, xs.at[1, p], rb.at[1, p], right)

    def last_left(p):
        return remote(base + 6 * RS + p, xs.at[0, p], rb.at[0, p], left)

    def loop(start, stop, act):
        def one(d, _):
            act(d)
            return 0

        lax.fori_loop(start, stop, one, 0)

    local[0].wait()
    own_right(0).start()
    own_left(AG - 1).start()
    own_twin.start()

    def own(i):
        own_right(i).start()
        own_left(AG - 1 - i).start()

    loop(1, AG, own)

    def block_copy(d):
        return pltpu.make_async_remote_copy(
            src_ref=stage.at[d], dst_ref=recv.at[d], send_sem=fsem.at[d], recv_sem=frsem.at[d],
            device_id=(r, peer(d)), device_id_type=MESH,
        )

    def picked(d):
        return fo[lists_s[peer(d)]]

    recv[0] = picked(0)

    def send_block(d, _):
        stage[d] = picked(d)
        block_copy(d).start()
        return 0

    lax.fori_loop(1, ncol, send_block, 0)

    def dense_all(slot, fresh):
        rows = nodes // 2
        src = fo if slot == 0 else fg.at[slot - 1]

        def one(i):
            at = pl.ds(pl.multiple_of(i * rows, rows), rows)
            v = mm(st[slot, at, :], src[...].reshape(nodes, -1))
            y[at, :] = v if fresh else y[at, :] + v

        loop(0, 2, one)

    stripes[0].wait()
    dense_all(0, True)
    stripes[1].wait()
    own_twin.wait_recv()
    dense_all(1, False)
    for k in range(2, 8):
        stripes[k].wait()

    scan[0] = jnp.zeros((blk, blk), F32)

    def same(row, j):
        return meta_s[row, j].astype(F32)

    def sparse_forward():
        meta_copy.wait()
        local[2].wait()

        def wait_block(d, _):
            block_copy(d).wait_recv()
            return 0

        lax.fori_loop(1, ncol, wait_block, 0)

        def step(j):
            t = meta_s[0, j]
            d = lax.rem(c + ncol - slots_s[t], ncol)
            scan[j + 1] = mm(tv[t], recv[d]) + same(3, j) * scan[j]

        loop(0, nt, step)

        def put(k):
            y[pl.ds(pl.multiple_of(k * blk, blk), blk), :] += scan[meta_s[2, k]]

        loop(0, nblk, put)

    def add(slot, p):
        lo = pl.multiple_of(p * piece, piece)
        rows = nodes // 2

        def one(i):
            at = pl.ds(pl.multiple_of(i * rows, rows), rows)
            y[at, :] += mm(st[slot, at, pl.ds(lo, piece)], fg[slot - 1, pl.ds(p * pb, pb)].reshape(piece, -1))

        loop(0, 2, one)

    def near(i, onward):
        j = AG - 1 - i
        own_right(i).wait_recv()
        if onward:
            on_right(i).start()
        to_twin(2, i).start()
        own_left(j).wait_recv()
        if onward:
            on_left(j).start()
        to_twin(4, j).start()
        add(2, i)
        add(4, j)
        to_twin(2, i).wait_recv()
        add(3, i)
        to_twin(4, j).wait_recv()
        add(5, j)

    def distant(i):
        j = AG - 1 - i
        on_right(i).wait_recv()
        to_twin(6, i).start()
        on_left(j).wait_recv()
        to_twin(6, j).start()
        add(6, i)
        add(6, j)
        to_twin(6, i).wait_recv()
        add(7, i)
        to_twin(6, j).wait_recv()
        add(7, j)

    loop(0, half, lambda i: near(i, True))
    sparse_forward()
    loop(half, AG, lambda i: near(i, False))
    loop(0, half, distant)

    local[1].wait()
    w = weight[...]
    chunk = 2 * blk
    biasp[...] = jnp.zeros_like(biasp)

    def pointwise(k):
        s = pl.ds(pl.multiple_of(k * chunk, chunk), chunk)
        yk = y[s, :].astype(BF16)
        yb[s, :] = yk
        x = mm(yk, w) + bias[...]
        g = jax.nn.sigmoid(x)
        hid[s, :] = (x * g).astype(BF16)
        gk = (cv[s, :].astype(F32) * (g * (1.0 + x * (1.0 - g)))).astype(BF16)
        gp[s, :] = gk
        biasp[...] += jnp.sum(gk.astype(F32).reshape(chunk // 8, 8, blk), axis=0)
        gtk = lax.dot_general(w, gk, (((1,), (1,)), ((), ())), preferred_element_type=F32).astype(BF16)
        gt[:, s] = gtk
        for h in range(2):
            gtb[2 * k + h] = gtk[:, h * blk:(h + 1) * blk]

    loop(0, nodes // chunk, pointwise)
    hid_copy = pltpu.make_async_copy(hid, hid_out, lsem.at[12])
    hid_copy.start()

    def back(slot, p):
        return mm(gt[...], st[slot, :, pl.ds(pl.multiple_of(p * width, width), width)])

    def send_sib(q):
        def one(p):
            ps[q, p] = back(2 * q + 1, p).astype(BF16)
            give(q, p).start()

        loop(0, RS, one)

    def keep_own(q):
        def one(p):
            pa[q, p] = back(2 * q, p)

        loop(0, RS, one)

    def summed(q, p):
        give(q, p).wait_recv()
        return pa[q, p] + sr[q, p].astype(F32)

    send_sib(3)
    keep_own(3)
    send_sib(2)

    def first(i):
        j = RS - 1 - i
        xs[2, i] = summed(3, i).astype(BF16)
        first_right(i).start()
        xs[2, j] = summed(3, j).astype(BF16)
        first_left(j).start()

    loop(0, rhalf, first)
    send_sib(1)

    gw = lax.dot_general(yb[...], gp[...], (((0,), (0,)), ((), ())), preferred_element_type=F32)
    wrows = blk // ncol
    for q in range(ncol):
        gws[q, 0:wrows] = gw[q * wrows:(q + 1) * wrows, :]
        gws[q, wrows:wrows + 8] = biasp[...]

    def a1(d):
        return pltpu.make_async_remote_copy(
            src_ref=gws.at[peer(d)], dst_ref=gwr.at[d], send_sem=a1s.at[d], recv_sem=a1r.at[d],
            device_id=(r, peer(d)), device_id_type=MESH,
        )

    def a2(d):
        return pltpu.make_async_remote_copy(
            src_ref=g2s, dst_ref=g2r.at[d], send_sem=a2s.at[d], recv_sem=a2r.at[d],
            device_id=(lax.rem(r + d, nrow), c), device_id_type=MESH,
        )

    def a3(d, owner):
        return pltpu.make_async_remote_copy(
            src_ref=gwo.at[owner], dst_ref=gwo.at[owner], send_sem=a3s.at[d], recv_sem=a3r.at[d],
            device_id=(r, peer(d)), device_id_type=MESH,
        )

    def run(n, act):
        loop(1, n, act)

    run(ncol, lambda d: a1(d).start())

    def back_copy(d):
        return pltpu.make_async_remote_copy(
            src_ref=bst.at[d], dst_ref=brecv.at[d], send_sem=bsem.at[d], recv_sem=brsem.at[d],
            device_id=(r, lax.rem(c + ncol - d, ncol)), device_id_type=MESH,
        )

    def bstep(j):
        t = meta_s[8, j]
        scan[j + 1] = mm(gtb[rows_s[t]], tv[t]) + same(11, j) * scan[j]

    loop(0, nt, bstep)

    def slot_sum(d):
        return scan[meta_s[10, d]].astype(BF16)

    brecv[0] = slot_sum(0)

    def send_back(d, _):
        bst[d] = slot_sum(d)
        back_copy(d).start()
        return 0

    lax.fori_loop(1, ncol, send_back, 0)

    keep_own(2)
    keep_own(1)

    def direct(i):
        j = RS - 1 - i
        xs[1, j] = summed(2, j).astype(BF16)
        last_right(j).start()
        xs[0, i] = summed(1, i).astype(BF16)
        last_left(i).start()

    loop(0, rhalf, direct)
    send_sib(0)
    keep_own(0)

    run(ncol, lambda d: a1(d).wait_recv())
    part2 = gws[c]
    for d in range(1, ncol):
        part2 += gwr[d]
    g2s[...] = part2
    run(nrow, lambda d: a2(d).start())

    def relay(i):
        j = RS - 1 - i
        first_right(i).wait_recv()
        xs[1, i] = (summed(2, i) + ra[i].astype(F32)).astype(BF16)
        last_right(i).start()
        first_left(j).wait_recv()
        xs[0, j] = (summed(1, j) + ra[j].astype(F32)).astype(BF16)
        last_left(j).start()

    loop(0, rhalf, relay)

    run(ncol, lambda d: back_copy(d).wait_recv())

    def rstep(j):
        scan[j + 1] = brecv[meta_s[16, j]].astype(F32) + same(19, j) * scan[j]

    loop(0, ncol, rstep)

    run(nrow, lambda d: a2(d).wait_recv())
    part3 = g2s[...]
    for d in range(1, nrow):
        part3 += g2r[d]
    gwo[c] = part3[0:wrows] * scale
    gb_out[...] = jnp.sum(part3[wrows:wrows + 8], axis=0, keepdims=True) * scale
    run(ncol, lambda d: a3(d, c).start())

    per = width // blk

    def gf_copy(p):
        s = pl.ds(pl.multiple_of(p * width, width), width)
        return pltpu.make_async_copy(gfv.at[s], gf_out.at[s], lsem.at[13 + p])

    def finish(p):
        total = summed(0, p)
        last_right(p).wait_recv()
        last_left(p).wait_recv()
        total = total + rb[0, p].astype(F32) + rb[1, p].astype(F32)
        for h in range(per):
            k = p * per + h
            block = total[:, h * blk:(h + 1) * blk] + scan[meta_s[18, k]]
            gfv[pl.ds(pl.multiple_of(k * blk, blk), blk), :] = block.T.astype(BF16)
        gf_copy(p).start()

    loop(0, RS, finish)

    run(ncol, lambda d: a3(d, lax.rem(c + ncol - d, ncol)).wait_recv())
    gw_out[...] = gwo[...].reshape(gw_out.shape)

    def ag_sent(p):
        own_right(p).wait_send()
        own_left(p).wait_send()
        for slot in (2, 4, 6):
            to_twin(slot, p).wait_send()
        on_right(p).wait_send()

    own_twin.wait_send()
    loop(0, AG, ag_sent)

    def rs_sent(p):
        for q in range(4):
            give(q, p).wait_send()
        first_right(p).wait_send()
        last_right(p).wait_send()
        last_left(p).wait_send()

    loop(0, RS, rs_sent)
    run(ncol, lambda d: block_copy(d).wait_send())
    run(ncol, lambda d: back_copy(d).wait_send())
    run(ncol, lambda d: a1(d).wait_send())
    run(nrow, lambda d: a2(d).wait_send())
    run(ncol, lambda d: a3(d, c).wait_send())
    hid_copy.wait()
    loop(0, RS, lambda p: gf_copy(p).wait())


def solution(mesh):
    nrow, ncol = mesh.shape["row"], mesh.shape["col"]

    def body(features, weight, bias_vector, stripe_values, tile_values, tile_rows, tile_slots, send_lists, cotangent):
        nodes, f = features.shape
        nt, blk, _ = tile_values.shape
        nblk = nodes // blk
        wrows = blk // ncol
        scale = 1.0 / math.sqrt(nodes * nrow * ncol)
        vm = pltpu.VMEM
        dma = pltpu.SemaphoreType.DMA
        copies = 6 * AG + 1 + 7 * RS
        any_, vmem, smem = (pl.BlockSpec(memory_space=m) for m in (pl.ANY, pltpu.VMEM, pltpu.SMEM))
        hid, gf, gw, gb = pl.pallas_call(
            functools.partial(kernel, nrow, ncol, scale),
            out_shape=(
                jax.ShapeDtypeStruct((nodes, f), BF16),
                jax.ShapeDtypeStruct((nodes, f), BF16),
                jax.ShapeDtypeStruct((f, f), F32),
                jax.ShapeDtypeStruct((1, f), F32),
            ),
            in_specs=[any_, vmem, vmem, any_, any_, smem, smem, smem, any_],
            out_specs=(any_, any_, vmem, vmem),
            scratch_shapes=[
                vm((8, nodes, nodes), BF16),
                vm((nblk, blk, f), BF16),
                vm((7, nblk, blk, f), BF16),
                vm((nt, blk, blk), BF16),
                vm((nodes, f), BF16),
                vm((ncol, blk, f), BF16),
                vm((ncol, blk, f), BF16),
                vm((24, 128), jnp.int32),
                pltpu.SMEM((24, 128), jnp.int32),
                vm((nt + 1, blk, blk), F32),
                vm((nodes, f), F32),
                vm((nodes, f), BF16),
                vm((nodes, f), BF16),
                vm((nodes, f), BF16),
                vm((f, nodes), BF16),
                vm((nblk, f, blk), BF16),
                vm((4, RS, f, nodes // RS), F32),
                vm((4, RS, f, nodes // RS), BF16),
                vm((4, RS, f, nodes // RS), BF16),
                vm((3, RS, f, nodes // RS), BF16),
                vm((RS, f, nodes // RS), BF16),
                vm((2, RS, f, nodes // RS), BF16),
                vm((ncol, f, blk), BF16),
                vm((ncol, f, blk), BF16),
                vm((ncol, wrows + 8, f), F32),
                vm((ncol, wrows + 8, f), F32),
                vm((wrows + 8, f), F32),
                vm((nrow, wrows + 8, f), F32),
                vm((ncol, wrows, f), F32),
                vm((nodes, f), BF16),
                vm((8, f), F32),
                dma((13 + RS,)),
                dma((copies,)), dma((copies,)),
                dma((ncol,)), dma((ncol,)), dma((ncol,)), dma((ncol,)),
                dma((ncol,)), dma((ncol,)), dma((nrow,)), dma((nrow,)), dma((ncol,)), dma((ncol,)),
            ],
            compiler_params=pltpu.CompilerParams(
                collective_id=0, has_side_effects=True, vmem_limit_bytes=56 * 2**20
            ),
        )(
            features.reshape(nblk, blk, f), weight, bias_vector.reshape(1, f), stripe_values, tile_values,
            tile_rows, tile_slots, send_lists.reshape(ncol), cotangent,
        )
        return hid, gf, gw, gb.reshape(f)

    return jax.shard_map(
        body,
        mesh=mesh,
        in_specs=(
            P(("row", "col"), None),
            P(),
            P(),
            P(("row", "col"), None),
            P(("row", "col"), None, None),
            P(("row", "col")),
            P(("row", "col")),
            P("row", "col", None, None),
            P(("row", "col"), None),
        ),
        out_specs=(P(("row", "col"), None), P(("row", "col"), None), P(), P()),
        check_vma=False,
    )
```

```python
import functools
import math

import jax
import jax.numpy as jnp
from jax import lax
from jax.experimental import pallas as pl
from jax.experimental.pallas import tpu as pltpu
from jax.sharding import PartitionSpec as P

MESH = pl.DeviceIdType.MESH
BF16 = jnp.bfloat16
F32 = jnp.float32
AG = 4
RS = 4


def mm(a, b):
    return jnp.dot(a, b, preferred_element_type=F32)


def order(read, n, lanes=128):
    sub = lax.broadcasted_iota(jnp.int32, (n, lanes), 0)
    lane = lax.broadcasted_iota(jnp.int32, (n, lanes), 1)
    col = jnp.zeros((n, lanes), jnp.int32)
    row = jnp.full((n, lanes), 1 << 20, jnp.int32)

    def one(t, both):
        v = read(t)
        return jnp.where(sub == t, v, both[0]), jnp.where(lane == t, v * n + t, both[1])

    col, row = lax.fori_loop(0, n, one, (col, row))
    less = (row < col * n + sub).astype(jnp.int32)
    rank = jnp.sum(less, axis=1, keepdims=True)
    hit = rank == lane
    perm = jnp.sum(jnp.where(hit, sub, 0), axis=0, keepdims=True)
    value = jnp.sum(jnp.where(hit, col, 0), axis=0, keepdims=True)
    last = jnp.sum((col <= lane).astype(jnp.int32), axis=0, keepdims=True)
    count = jnp.sum((col == lane).astype(jnp.int32), axis=0, keepdims=True)
    last = jnp.where(count > 0, last, 0)
    before = jnp.sum(((row // n == col) & (lane < sub)).astype(jnp.int32), axis=1, keepdims=True)
    again = jnp.sum(jnp.where(hit & (before > 0), 1, 0), axis=0, keepdims=True)
    return jnp.concatenate([perm, value, last, again] + [jnp.zeros_like(perm)] * 4, axis=0)


def kernel(
    nrow, ncol, scale,
    feat, weight, bias, stripe, tiles, rows_s, slots_s, lists_s, cot,
    hid_out, gf_out, gw_out, gb_out,
    st, fo, fg, tv, cv, recv, stage, meta_v, meta_s, scan, y, yb, gp, hid, gt, gtb,
    pa, ps, sr, xs, ra, rb, bst, brecv, gws, gwr, g2s, g2r, gwo, gfv, biasp,
    lsem, ssem, rsem, fsem, frsem, bsem, brsem, heard, a1s, a1r, a2s, a2r, a3s, a3r,
):
    nblk, blk, _ = feat.shape
    nt = tv.shape[0]
    nodes = nblk * blk
    r = lax.axis_index("row")
    c = lax.axis_index("col")
    chip, core = r // 2, r % 2
    chips = nrow // 2
    chip_r, chip_l, chip_f = (chip + 1) % chips, (chip + chips - 1) % chips, (chip + 2) % chips
    sib = chip * 2 + 1 - core
    right, left = chip_r * 2 + core, chip_l * 2 + core
    order_of = [
        chip * 2 + core, chip * 2 + 1 - core,
        chip_l * 2 + core, chip_l * 2 + 1 - core,
        chip_r * 2 + core, chip_r * 2 + 1 - core,
        chip_f * 2 + core, chip_f * 2 + 1 - core,
    ]

    def peer(d):
        return lax.rem(c + d, ncol)

    local = [
        pltpu.make_async_copy(feat, fo, lsem.at[8]),
        pltpu.make_async_copy(cot, cv, lsem.at[9]),
        pltpu.make_async_copy(tiles, tv, lsem.at[10]),
    ]
    local[0].start()
    stripes = [
        pltpu.make_async_copy(
            stripe.at[:, pl.ds(pl.multiple_of(order_of[k] * nodes, 128), nodes)], st.at[k], lsem.at[k]
        )
        for k in range(8)
    ]
    stripes[0].start()
    stripes[1].start()
    local[2].start()
    barrier = pltpu.get_barrier_semaphore()

    side = next(k for k in range(1, ncol + 1) if k * k >= ncol)
    cy, cz = c // side, c % side
    others = [(row, c) for row in (sib, right, left)]
    z_peers = [(r, cy * side + (cz + d) % side) for d in range(1, side)]
    y_peers = [(r, (cy + d) % (ncol // side) * side + cz) for d in range(1, ncol // side)]
    for dev in others + z_peers + y_peers:
        pl.semaphore_signal(barrier, inc=1, device_id=dev, device_id_type=MESH)

    meta_v[0:8] = order(lambda t: rows_s[t], nt)
    meta_v[8:16] = order(lambda t: lax.rem(c + ncol - slots_s[t], ncol), nt)
    meta_v[16:24] = order(lambda d: lists_s[peer(d)], ncol)
    meta_copy = pltpu.make_async_copy(meta_v, meta_s, lsem.at[11])
    meta_copy.start()

    pl.semaphore_wait(barrier, len(others + z_peers + y_peers))
    for dev in z_peers:
        pl.semaphore_signal(heard, inc=1, device_id=dev, device_id_type=MESH)

    piece, half = nodes // AG, AG // 2
    pb = piece // blk
    width, rhalf = nodes // RS, RS // 2

    def remote(i, src, dst, row):
        return pltpu.make_async_remote_copy(
            src_ref=src, dst_ref=dst, send_sem=ssem.at[i], recv_sem=rsem.at[i],
            device_id=(row, c), device_id_type=MESH,
        )

    def part(slot, p):
        own = fo if slot == 0 else fg.at[slot - 1]
        return own.at[pl.ds(p * pb, pb)]

    def own_right(p):
        return remote(p, part(0, p), part(2, p), right)

    def own_left(p):
        return remote(AG + p, part(0, p), part(4, p), left)

    def on_right(p):
        return remote(2 * AG + p, part(2, p), part(6, p), right)

    def on_left(p):
        return remote(2 * AG + p, part(4, p), part(6, p), left)

    def to_twin(slot, p):
        return remote(3 * AG + (slot - 2) // 2 * AG + p, part(slot, p), part(slot + 1, p), sib)

    own_twin = remote(6 * AG, fo, fg.at[0], sib)
    base = 6 * AG + 1

    def give(q, p):
        return remote(base + q * RS + p, ps.at[q, p], sr.at[q, p], sib)

    def first_right(p):
        return remote(base + 4 * RS + p, xs.at[2, p], ra.at[p], right)

    def first_left(p):
        return remote(base + 4 * RS + p, xs.at[2, p], ra.at[p], left)

    def last_right(p):
        return remote(base + 5 * RS + p, xs.at[1, p], rb.at[1, p], right)

    def last_left(p):
        return remote(base + 6 * RS + p, xs.at[0, p], rb.at[0, p], left)

    def loop(start, stop, act):
        def one(d, _):
            act(d)
            return 0

        lax.fori_loop(start, stop, one, 0)

    local[0].wait()
    own_right(0).start()
    own_left(AG - 1).start()
    own_twin.start()

    def own(i):
        own_right(i).start()
        own_left(AG - 1 - i).start()

    loop(1, AG, own)
    for k in range(2, 8):
        stripes[k].start()
    local[1].start()

    def block_copy(d):
        return pltpu.make_async_remote_copy(
            src_ref=stage.at[d], dst_ref=recv.at[d], send_sem=fsem.at[d], recv_sem=frsem.at[d],
            device_id=(r, peer(d)), device_id_type=MESH,
        )

    def picked(d):
        return fo[lists_s[peer(d)]]

    pl.semaphore_wait(heard, len(z_peers))
    recv[0] = picked(0)

    def send_block(d, _):
        stage[d] = picked(d)
        block_copy(d).start()
        return 0

    lax.fori_loop(1, ncol, send_block, 0)

    def dense_all(slot, fresh):
        rows = nodes // 2
        src = fo if slot == 0 else fg.at[slot - 1]

        def one(i):
            at = pl.ds(pl.multiple_of(i * rows, rows), rows)
            v = mm(st[slot, at, :], src[...].reshape(nodes, -1))
            y[at, :] = v if fresh else y[at, :] + v

        loop(0, 2, one)

    stripes[0].wait()
    dense_all(0, True)
    stripes[1].wait()
    own_twin.wait_recv()
    dense_all(1, False)
    for k in range(2, 8):
        stripes[k].wait()

    scan[0] = jnp.zeros((blk, blk), F32)

    def same(row, j):
        return meta_s[row, j].astype(F32)

    unroll = 4

    def scan_loop(n, row, term):
        def step(i):
            terms = [term(i * unroll + u) for u in range(unroll)]
            run_sum = scan[i * unroll]
            for u in range(unroll):
                run_sum = terms[u] + same(row, i * unroll + u) * run_sum
                scan[i * unroll + u + 1] = run_sum

        loop(0, n // unroll, step)

    def sparse_forward():
        meta_copy.wait()
        local[2].wait()

        def wait_block(d, _):
            block_copy(d).wait_recv()
            return 0

        lax.fori_loop(1, ncol, wait_block, 0)

        def product(j):
            t = meta_s[0, j]
            return mm(tv[t], recv[lax.rem(c + ncol - slots_s[t], ncol)])

        scan_loop(nt, 3, product)

        def put(k):
            y[pl.ds(pl.multiple_of(k * blk, blk), blk), :] += scan[meta_s[2, k]]

        loop(0, nblk, put)

    def add(slot, p):
        lo = pl.multiple_of(p * piece, piece)
        rows = nodes // 2

        def one(i):
            at = pl.ds(pl.multiple_of(i * rows, rows), rows)
            y[at, :] += mm(st[slot, at, pl.ds(lo, piece)], fg[slot - 1, pl.ds(p * pb, pb)].reshape(piece, -1))

        loop(0, 2, one)

    def near(i, onward):
        j = AG - 1 - i
        own_right(i).wait_recv()
        if onward:
            on_right(i).start()
        to_twin(2, i).start()
        own_left(j).wait_recv()
        if onward:
            on_left(j).start()
        to_twin(4, j).start()
        add(2, i)
        add(4, j)
        to_twin(2, i).wait_recv()
        add(3, i)
        to_twin(4, j).wait_recv()
        add(5, j)

    def distant(i):
        j = AG - 1 - i
        on_right(i).wait_recv()
        to_twin(6, i).start()
        on_left(j).wait_recv()
        to_twin(6, j).start()
        add(6, i)
        add(6, j)
        to_twin(6, i).wait_recv()
        add(7, i)
        to_twin(6, j).wait_recv()
        add(7, j)

    loop(0, half, lambda i: near(i, True))
    loop(half, AG, lambda i: near(i, False))
    sparse_forward()
    loop(0, half, distant)

    local[1].wait()
    w = weight[...]
    chunk = 2 * blk
    biasp[...] = jnp.zeros_like(biasp)

    def pointwise(k):
        s = pl.ds(pl.multiple_of(k * chunk, chunk), chunk)
        yk = y[s, :].astype(BF16)
        yb[s, :] = yk
        x = mm(yk, w) + bias[...]
        g = jax.nn.sigmoid(x)
        hid[s, :] = (x * g).astype(BF16)
        gk = (cv[s, :].astype(F32) * (g * (1.0 + x * (1.0 - g)))).astype(BF16)
        gp[s, :] = gk
        biasp[...] += jnp.sum(gk.astype(F32).reshape(chunk // 8, 8, blk), axis=0)
        gtk = lax.dot_general(w, gk, (((1,), (1,)), ((), ())), preferred_element_type=F32).astype(BF16)
        gt[:, s] = gtk
        for h in range(2):
            gtb[2 * k + h] = gtk[:, h * blk:(h + 1) * blk]

    loop(0, nodes // chunk, pointwise)
    hid_copy = pltpu.make_async_copy(hid, hid_out, lsem.at[12])
    hid_copy.start()

    def back(slot, p):
        return mm(gt[...], st[slot, :, pl.ds(pl.multiple_of(p * width, width), width)])

    def send_sib(q):
        def one(p):
            ps[q, p] = back(2 * q + 1, p).astype(BF16)
            give(q, p).start()

        loop(0, RS, one)

    def keep_own(q):
        def one(p):
            pa[q, p] = back(2 * q, p)

        loop(0, RS, one)

    def summed(q, p):
        give(q, p).wait_recv()
        return pa[q, p] + sr[q, p].astype(F32)

    send_sib(3)
    keep_own(3)
    send_sib(2)

    def first(i):
        j = RS - 1 - i
        xs[2, i] = summed(3, i).astype(BF16)
        first_right(i).start()
        xs[2, j] = summed(3, j).astype(BF16)
        first_left(j).start()

    loop(0, rhalf, first)
    send_sib(1)

    gw = lax.dot_general(yb[...], gp[...], (((0,), (0,)), ((), ())), preferred_element_type=F32)
    wrows = blk // ncol
    for q in range(ncol):
        gws[q, 0:wrows] = gw[q * wrows:(q + 1) * wrows, :]
        gws[q, wrows:wrows + 8] = biasp[...]

    def a1(d):
        return pltpu.make_async_remote_copy(
            src_ref=gws.at[peer(d)], dst_ref=gwr.at[d], send_sem=a1s.at[d], recv_sem=a1r.at[d],
            device_id=(r, peer(d)), device_id_type=MESH,
        )

    def a2(d):
        return pltpu.make_async_remote_copy(
            src_ref=g2s, dst_ref=g2r.at[d], send_sem=a2s.at[d], recv_sem=a2r.at[d],
            device_id=(lax.rem(r + d, nrow), c), device_id_type=MESH,
        )

    def a3(d, owner):
        return pltpu.make_async_remote_copy(
            src_ref=gwo.at[owner], dst_ref=gwo.at[owner], send_sem=a3s.at[d], recv_sem=a3r.at[d],
            device_id=(r, peer(d)), device_id_type=MESH,
        )

    def run(n, act):
        loop(1, n, act)

    run(ncol, lambda d: a1(d).start())

    def back_copy(d):
        return pltpu.make_async_remote_copy(
            src_ref=bst.at[d], dst_ref=brecv.at[d], send_sem=bsem.at[d], recv_sem=brsem.at[d],
            device_id=(r, lax.rem(c + ncol - d, ncol)), device_id_type=MESH,
        )

    def bproduct(j):
        t = meta_s[8, j]
        return mm(gtb[rows_s[t]], tv[t])

    scan_loop(nt, 11, bproduct)

    def slot_sum(d):
        return scan[meta_s[10, d]].astype(BF16)

    brecv[0] = slot_sum(0)

    def send_back(d, _):
        bst[d] = slot_sum(d)
        back_copy(d).start()
        return 0

    lax.fori_loop(1, ncol, send_back, 0)

    keep_own(2)
    keep_own(1)

    def direct(i):
        j = RS - 1 - i
        xs[1, j] = summed(2, j).astype(BF16)
        last_right(j).start()
        xs[0, i] = summed(1, i).astype(BF16)
        last_left(i).start()

    loop(0, rhalf, direct)
    send_sib(0)
    keep_own(0)

    run(ncol, lambda d: a1(d).wait_recv())
    part2 = gws[c]
    for d in range(1, ncol):
        part2 += gwr[d]
    g2s[...] = part2
    run(nrow, lambda d: a2(d).start())

    def relay(i):
        j = RS - 1 - i
        first_right(i).wait_recv()
        xs[1, i] = (summed(2, i) + ra[i].astype(F32)).astype(BF16)
        last_right(i).start()
        first_left(j).wait_recv()
        xs[0, j] = (summed(1, j) + ra[j].astype(F32)).astype(BF16)
        last_left(j).start()

    loop(0, rhalf, relay)

    run(ncol, lambda d: back_copy(d).wait_recv())

    scan_loop(ncol, 19, lambda j: brecv[meta_s[16, j]].astype(F32))

    run(nrow, lambda d: a2(d).wait_recv())
    part3 = g2s[...]
    for d in range(1, nrow):
        part3 += g2r[d]
    gwo[c] = part3[0:wrows] * scale
    gb_out[...] = jnp.sum(part3[wrows:wrows + 8], axis=0, keepdims=True) * scale
    run(ncol, lambda d: a3(d, c).start())

    per = width // blk

    def gf_copy(p):
        s = pl.ds(pl.multiple_of(p * width, width), width)
        return pltpu.make_async_copy(gfv.at[s], gf_out.at[s], lsem.at[13 + p])

    def finish(p):
        total = summed(0, p)
        last_right(p).wait_recv()
        last_left(p).wait_recv()
        total = total + rb[0, p].astype(F32) + rb[1, p].astype(F32)
        for h in range(per):
            k = p * per + h
            block = total[:, h * blk:(h + 1) * blk] + scan[meta_s[18, k]]
            gfv[pl.ds(pl.multiple_of(k * blk, blk), blk), :] = block.T.astype(BF16)
        gf_copy(p).start()

    loop(0, RS, finish)

    run(ncol, lambda d: a3(d, lax.rem(c + ncol - d, ncol)).wait_recv())
    gw_out[...] = gwo[...].reshape(gw_out.shape)

    def ag_sent(p):
        own_right(p).wait_send()
        own_left(p).wait_send()
        for slot in (2, 4, 6):
            to_twin(slot, p).wait_send()
        on_right(p).wait_send()

    own_twin.wait_send()
    loop(0, AG, ag_sent)

    def rs_sent(p):
        for q in range(4):
            give(q, p).wait_send()
        first_right(p).wait_send()
        last_right(p).wait_send()
        last_left(p).wait_send()

    loop(0, RS, rs_sent)
    run(ncol, lambda d: block_copy(d).wait_send())
    run(ncol, lambda d: back_copy(d).wait_send())
    run(ncol, lambda d: a1(d).wait_send())
    run(nrow, lambda d: a2(d).wait_send())
    run(ncol, lambda d: a3(d, c).wait_send())
    hid_copy.wait()
    loop(0, RS, lambda p: gf_copy(p).wait())


def hand_over(*refs):
    sems = refs[-1]
    copies = [pltpu.make_async_copy(refs[i], refs[4 + i], sems.at[i]) for i in range(4)]
    for copy in copies:
        copy.start()
    for copy in copies:
        copy.wait()


def solution(mesh):
    nrow, ncol = mesh.shape["row"], mesh.shape["col"]

    def body(features, weight, bias_vector, stripe_values, tile_values, tile_rows, tile_slots, send_lists, cotangent):
        nodes, f = features.shape
        nt, blk, _ = tile_values.shape
        nblk = nodes // blk
        wrows = blk // ncol
        scale = 1.0 / math.sqrt(nodes * nrow * ncol)
        vm = pltpu.VMEM
        dma = pltpu.SemaphoreType.DMA
        copies = 6 * AG + 1 + 7 * RS
        any_, vmem, smem = (pl.BlockSpec(memory_space=m) for m in (pl.ANY, pltpu.VMEM, pltpu.SMEM))
        shapes = (
            jax.ShapeDtypeStruct((nodes, f), BF16),
            jax.ShapeDtypeStruct((nodes, f), BF16),
            jax.ShapeDtypeStruct((f, f), F32),
            jax.ShapeDtypeStruct((1, f), F32),
        )
        made = pl.pallas_call(
            functools.partial(kernel, nrow, ncol, scale),
            out_shape=shapes,
            in_specs=[any_, vmem, vmem, any_, any_, smem, smem, smem, any_],
            out_specs=(any_, any_, vmem, vmem),
            scratch_shapes=[
                vm((8, nodes, nodes), BF16),
                vm((nblk, blk, f), BF16),
                vm((7, nblk, blk, f), BF16),
                vm((nt, blk, blk), BF16),
                vm((nodes, f), BF16),
                vm((ncol, blk, f), BF16),
                vm((ncol, blk, f), BF16),
                vm((24, 128), jnp.int32),
                pltpu.SMEM((24, 128), jnp.int32),
                vm((nt + 1, blk, blk), F32),
                vm((nodes, f), F32),
                vm((nodes, f), BF16),
                vm((nodes, f), BF16),
                vm((nodes, f), BF16),
                vm((f, nodes), BF16),
                vm((nblk, f, blk), BF16),
                vm((4, RS, f, nodes // RS), F32),
                vm((4, RS, f, nodes // RS), BF16),
                vm((4, RS, f, nodes // RS), BF16),
                vm((3, RS, f, nodes // RS), BF16),
                vm((RS, f, nodes // RS), BF16),
                vm((2, RS, f, nodes // RS), BF16),
                vm((ncol, f, blk), BF16),
                vm((ncol, f, blk), BF16),
                vm((ncol, wrows + 8, f), F32),
                vm((ncol, wrows + 8, f), F32),
                vm((wrows + 8, f), F32),
                vm((nrow, wrows + 8, f), F32),
                vm((ncol, wrows, f), F32),
                vm((nodes, f), BF16),
                vm((8, f), F32),
                dma((13 + RS,)),
                dma((copies,)), dma((copies,)),
                dma((ncol,)), dma((ncol,)), dma((ncol,)), dma((ncol,)),
                pltpu.SemaphoreType.REGULAR,
                dma((ncol,)), dma((ncol,)), dma((nrow,)), dma((nrow,)), dma((ncol,)), dma((ncol,)),
            ],
            compiler_params=pltpu.CompilerParams(
                collective_id=0, has_side_effects=True, vmem_limit_bytes=56 * 2**20
            ),
        )(
            features.reshape(nblk, blk, f), weight, bias_vector.reshape(1, f), stripe_values, tile_values,
            tile_rows, tile_slots, send_lists.reshape(ncol), cotangent,
        )
        hid, gf, gw, gb = pl.pallas_call(
            hand_over, out_shape=shapes, in_specs=[vmem] * 4, out_specs=(any_,) * 4, scratch_shapes=[dma((4,))]
        )(*made)
        return hid, gf, gw, gb.reshape(f)

    return jax.shard_map(
        body,
        mesh=mesh,
        in_specs=(
            P(("row", "col"), None),
            P(),
            P(),
            P(("row", "col"), None),
            P(("row", "col"), None, None),
            P(("row", "col")),
            P(("row", "col")),
            P("row", "col", None, None),
            P(("row", "col"), None),
        ),
        out_specs=(P(("row", "col"), None), P(("row", "col"), None), P(), P()),
        check_vma=False,
    )
```

```python
import functools
import math

import jax
import jax.numpy as jnp
from jax import lax
from jax.experimental import pallas as pl
from jax.experimental.pallas import tpu as pltpu
from jax.sharding import PartitionSpec as P

MESH = pl.DeviceIdType.MESH
BF16 = jnp.bfloat16
F32 = jnp.float32
AG = 4
RS = 4


def mm(a, b):
    return jnp.dot(a, b, preferred_element_type=F32)


def order(read, n, lanes=128):
    sub = lax.broadcasted_iota(jnp.int32, (n, lanes), 0)
    lane = lax.broadcasted_iota(jnp.int32, (n, lanes), 1)
    col = jnp.zeros((n, lanes), jnp.int32)
    row = jnp.full((n, lanes), 1 << 20, jnp.int32)

    def one(t, both):
        v = read(t)
        return jnp.where(sub == t, v, both[0]), jnp.where(lane == t, v * n + t, both[1])

    col, row = lax.fori_loop(0, n, one, (col, row))
    less = (row < col * n + sub).astype(jnp.int32)
    rank = jnp.sum(less, axis=1, keepdims=True)
    hit = rank == lane
    perm = jnp.sum(jnp.where(hit, sub, 0), axis=0, keepdims=True)
    value = jnp.sum(jnp.where(hit, col, 0), axis=0, keepdims=True)
    last = jnp.sum((col <= lane).astype(jnp.int32), axis=0, keepdims=True)
    count = jnp.sum((col == lane).astype(jnp.int32), axis=0, keepdims=True)
    last = jnp.where(count > 0, last, 0)
    before = jnp.sum(((row // n == col) & (lane < sub)).astype(jnp.int32), axis=1, keepdims=True)
    again = jnp.sum(jnp.where(hit & (before > 0), 1, 0), axis=0, keepdims=True)
    return jnp.concatenate([perm, value, last, again] + [jnp.zeros_like(perm)] * 4, axis=0)


def kernel(
    nrow, ncol, scale,
    feat, weight, bias, stripe, tiles, rows_s, slots_s, lists_s, cot,
    hid_out, gf_out, gw_out, gb_out,
    st, fo, fg, tv, cv, recv, stage, meta_v, meta_s, scan, y, yb, gp, hid, gt, gtb,
    pa, ps, sr, xs, ra, rb, bst, brecv, gws, gwr, g2s, g2r, gwo, gfv, biasp,
    lsem, ssem, rsem, fsem, frsem, bsem, brsem, heard, a1s, a1r, a2s, a2r, a3s, a3r,
):
    nblk, blk, _ = feat.shape
    nt = tv.shape[0]
    nodes = nblk * blk
    r = lax.axis_index("row")
    c = lax.axis_index("col")
    chip, core = r // 2, r % 2
    chips = nrow // 2
    chip_r, chip_l, chip_f = (chip + 1) % chips, (chip + chips - 1) % chips, (chip + 2) % chips
    sib = chip * 2 + 1 - core
    right, left = chip_r * 2 + core, chip_l * 2 + core
    order_of = [
        chip * 2 + core, chip * 2 + 1 - core,
        chip_l * 2 + core, chip_l * 2 + 1 - core,
        chip_r * 2 + core, chip_r * 2 + 1 - core,
        chip_f * 2 + core, chip_f * 2 + 1 - core,
    ]

    def peer(d):
        return lax.rem(c + d, ncol)

    local = [
        pltpu.make_async_copy(feat, fo, lsem.at[8]),
        pltpu.make_async_copy(cot, cv, lsem.at[9]),
        pltpu.make_async_copy(tiles, tv, lsem.at[10]),
    ]
    local[0].start()
    stripes = [
        pltpu.make_async_copy(
            stripe.at[:, pl.ds(pl.multiple_of(order_of[k] * nodes, 128), nodes)], st.at[k], lsem.at[k]
        )
        for k in range(8)
    ]
    stripes[0].start()
    stripes[1].start()
    for k in range(2, 8):
        stripes[k].start()
    local[2].start()
    local[1].start()
    barrier = pltpu.get_barrier_semaphore()

    side = next(k for k in range(1, ncol + 1) if k * k >= ncol)
    cy, cz = c // side, c % side
    others = [(row, c) for row in (sib, right, left)]
    z_peers = [(r, cy * side + (cz + d) % side) for d in range(1, side)]
    y_peers = [(r, (cy + d) % (ncol // side) * side + cz) for d in range(1, ncol // side)]
    for dev in others + z_peers + y_peers:
        pl.semaphore_signal(barrier, inc=1, device_id=dev, device_id_type=MESH)

    meta_v[0:8] = order(lambda t: rows_s[t], nt)
    meta_v[8:16] = order(lambda t: lax.rem(c + ncol - slots_s[t], ncol), nt)
    meta_v[16:24] = order(lambda d: lists_s[peer(d)], ncol)
    meta_copy = pltpu.make_async_copy(meta_v, meta_s, lsem.at[11])
    meta_copy.start()

    pl.semaphore_wait(barrier, len(others + z_peers + y_peers))
    for dev in z_peers:
        pl.semaphore_signal(heard, inc=1, device_id=dev, device_id_type=MESH)

    piece, half = nodes // AG, AG // 2
    pb = piece // blk
    width, rhalf = nodes // RS, RS // 2

    def remote(i, src, dst, row):
        return pltpu.make_async_remote_copy(
            src_ref=src, dst_ref=dst, send_sem=ssem.at[i], recv_sem=rsem.at[i],
            device_id=(row, c), device_id_type=MESH,
        )

    def part(slot, p):
        own = fo if slot == 0 else fg.at[slot - 1]
        return own.at[pl.ds(p * pb, pb)]

    def own_right(p):
        return remote(p, part(0, p), part(2, p), right)

    def own_left(p):
        return remote(AG + p, part(0, p), part(4, p), left)

    def on_right(p):
        return remote(2 * AG + p, part(2, p), part(6, p), right)

    def on_left(p):
        return remote(2 * AG + p, part(4, p), part(6, p), left)

    def to_twin(slot, p):
        return remote(3 * AG + (slot - 2) // 2 * AG + p, part(slot, p), part(slot + 1, p), sib)

    own_twin = remote(6 * AG, fo, fg.at[0], sib)
    base = 6 * AG + 1

    def give(q, p):
        return remote(base + q * RS + p, ps.at[q, p], sr.at[q, p], sib)

    def first_right(p):
        return remote(base + 4 * RS + p, xs.at[2, p], ra.at[p], right)

    def first_left(p):
        return remote(base + 4 * RS + p, xs.at[2, p], ra.at[p], left)

    def last_right(p):
        return remote(base + 5 * RS + p, xs.at[1, p], rb.at[1, p], right)

    def last_left(p):
        return remote(base + 6 * RS + p, xs.at[0, p], rb.at[0, p], left)

    def loop(start, stop, act):
        def one(d, _):
            act(d)
            return 0

        lax.fori_loop(start, stop, one, 0)

    local[0].wait()
    own_right(0).start()
    own_left(AG - 1).start()
    own_twin.start()

    def own(i):
        own_right(i).start()
        own_left(AG - 1 - i).start()

    loop(1, AG, own)
    def block_copy(d):
        return pltpu.make_async_remote_copy(
            src_ref=stage.at[d], dst_ref=recv.at[d], send_sem=fsem.at[d], recv_sem=frsem.at[d],
            device_id=(r, peer(d)), device_id_type=MESH,
        )

    def picked(d):
        return fo[lists_s[peer(d)]]

    def send_block(d):
        stage[d] = picked(d)
        block_copy(d).start()

    def send_blocks():
        pl.semaphore_wait(heard, len(z_peers))
        recv[0] = picked(0)
        loop(1, ncol, send_block)

    def dense_all(slot, fresh):
        rows = nodes // 2
        src = fo if slot == 0 else fg.at[slot - 1]

        def one(i):
            at = pl.ds(pl.multiple_of(i * rows, rows), rows)
            v = mm(st[slot, at, :], src[...].reshape(nodes, -1))
            y[at, :] = v if fresh else y[at, :] + v

        loop(0, 2, one)

    stripes[0].wait()
    dense_all(0, True)
    stripes[1].wait()
    own_twin.wait_recv()
    dense_all(1, False)
    scan[0] = jnp.zeros((blk, blk), F32)

    def same(row, j):
        return meta_s[row, j].astype(F32)

    unroll = 4

    def scan_loop(n, row, term):
        def step(i):
            terms = [term(i * unroll + u) for u in range(unroll)]
            run_sum = scan[i * unroll]
            for u in range(unroll):
                run_sum = terms[u] + same(row, i * unroll + u) * run_sum
                scan[i * unroll + u + 1] = run_sum

        loop(0, n // unroll, step)

    def sparse_forward():
        meta_copy.wait()
        local[2].wait()

        def wait_block(d, _):
            block_copy(d).wait_recv()
            return 0

        lax.fori_loop(1, ncol, wait_block, 0)

        def product(j):
            t = meta_s[0, j]
            return mm(tv[t], recv[lax.rem(c + ncol - slots_s[t], ncol)])

        scan_loop(nt, 3, product)

        def put(k):
            y[pl.ds(pl.multiple_of(k * blk, blk), blk), :] += scan[meta_s[2, k]]

        loop(0, nblk, put)

    def add(one, p, two, q):
        rows = nodes // 2

        def half_rows(i):
            at = pl.ds(pl.multiple_of(i * rows, rows), rows)
            parts = [
                mm(st[slot, at, u * piece:(u + 1) * piece], fg[slot - 1, u * pb:(u + 1) * pb].reshape(piece, -1))
                for slot, u in ((one, p), (two, q))
            ]
            y[at, :] += parts[0] + parts[1]

        loop(0, 2, half_rows)

    def arrive(i):
        j = AG - 1 - i
        own_right(i).wait_recv()
        if i < half:
            on_right(i).start()
        to_twin(2, i).start()
        own_left(j).wait_recv()
        if i < half:
            on_left(j).start()
        to_twin(4, j).start()

    def twins(i):
        j = AG - 1 - i
        to_twin(2, i).wait_recv()
        to_twin(4, j).wait_recv()
        add(3, i, 5, j)

    def arrive_far(i):
        j = AG - 1 - i
        on_right(i).wait_recv()
        to_twin(6, i).start()
        on_left(j).wait_recv()
        to_twin(6, j).start()

    def far_twins(i):
        j = AG - 1 - i
        to_twin(6, i).wait_recv()
        to_twin(6, j).wait_recv()
        add(7, i, 7, j)

    for i in range(AG):
        arrive(i)
        if i == 0:
            send_blocks()
            stripes[2].wait()
            stripes[4].wait()
        add(2, i, 4, AG - 1 - i)
        if i == 0:
            stripes[3].wait()
            stripes[5].wait()
        else:
            twins(i - 1)
    twins(AG - 1)
    stripes[6].wait()
    stripes[7].wait()
    for i in range(half):
        arrive_far(i)
        add(6, i, 6, AG - 1 - i)
        if i == 0:
            sparse_forward()
        else:
            far_twins(i - 1)
    far_twins(half - 1)

    local[1].wait()
    w = weight[...]
    chunk = 4 * blk
    biasp[...] = jnp.zeros_like(biasp)

    def pointwise(k):
        s = pl.ds(pl.multiple_of(k * chunk, chunk), chunk)
        yk = y[s, :].astype(BF16)
        yb[s, :] = yk
        x = mm(yk, w) + bias[...]
        g = jax.nn.sigmoid(x)
        hid[s, :] = (x * g).astype(BF16)
        gk = (cv[s, :].astype(F32) * (g * (1.0 + x * (1.0 - g)))).astype(BF16)
        gp[s, :] = gk
        biasp[...] += jnp.sum(gk.astype(F32).reshape(chunk // 8, 8, blk), axis=0)
        gtk = lax.dot_general(w, gk, (((1,), (1,)), ((), ())), preferred_element_type=F32).astype(BF16)
        gt[:, s] = gtk
        for h in range(4):
            gtb[4 * k + h] = gtk[:, h * blk:(h + 1) * blk]

    loop(0, nodes // chunk, pointwise)
    hid_copy = pltpu.make_async_copy(hid, hid_out, lsem.at[12])
    hid_copy.start()

    group = min(2, RS)

    def back(slot, i):
        wide = group * width
        return mm(gt[...], st[slot, :, pl.ds(pl.multiple_of(i * wide, wide), wide)])

    def send_sib(q):
        def one(i):
            v = back(2 * q + 1, i).astype(BF16)
            for u in range(group):
                ps[q, i * group + u] = v[:, u * width:(u + 1) * width]
                give(q, i * group + u).start()

        loop(0, RS // group, one)

    def keep_own(q):
        def one(i):
            v = back(2 * q, i)
            for u in range(group):
                pa[q, i * group + u] = v[:, u * width:(u + 1) * width]

        loop(0, RS // group, one)

    def summed(q, p):
        give(q, p).wait_recv()
        return pa[q, p] + sr[q, p].astype(F32)

    send_sib(3)

    gw = lax.dot_general(yb[...], gp[...], (((0,), (0,)), ((), ())), preferred_element_type=F32)
    wrows = blk // ncol
    for q in range(ncol):
        gws[q, 0:wrows] = gw[q * wrows:(q + 1) * wrows, :]
        gws[q, wrows:wrows + 8] = biasp[...]

    def a1(d):
        return pltpu.make_async_remote_copy(
            src_ref=gws.at[peer(d)], dst_ref=gwr.at[d], send_sem=a1s.at[d], recv_sem=a1r.at[d],
            device_id=(r, peer(d)), device_id_type=MESH,
        )

    def a2(d):
        return pltpu.make_async_remote_copy(
            src_ref=g2s, dst_ref=g2r.at[d], send_sem=a2s.at[d], recv_sem=a2r.at[d],
            device_id=(lax.rem(r + d, nrow), c), device_id_type=MESH,
        )

    def a3(d, owner):
        return pltpu.make_async_remote_copy(
            src_ref=gwo.at[owner], dst_ref=gwo.at[owner], send_sem=a3s.at[d], recv_sem=a3r.at[d],
            device_id=(r, peer(d)), device_id_type=MESH,
        )

    def run(n, act):
        loop(1, n, act)

    run(ncol, lambda d: a1(d).start())

    keep_own(3)

    def first(i):
        j = RS - 1 - i
        xs[2, i] = summed(3, i).astype(BF16)
        first_right(i).start()
        xs[2, j] = summed(3, j).astype(BF16)
        first_left(j).start()

    loop(0, rhalf, first)

    def back_copy(d):
        return pltpu.make_async_remote_copy(
            src_ref=bst.at[d], dst_ref=brecv.at[d], send_sem=bsem.at[d], recv_sem=brsem.at[d],
            device_id=(r, lax.rem(c + ncol - d, ncol)), device_id_type=MESH,
        )

    def bproduct(j):
        t = meta_s[8, j]
        return mm(gtb[rows_s[t]], tv[t])

    scan_loop(nt, 11, bproduct)

    def slot_sum(d):
        return scan[meta_s[10, d]].astype(BF16)

    brecv[0] = slot_sum(0)

    def send_back(d, _):
        bst[d] = slot_sum(d)
        back_copy(d).start()
        return 0

    lax.fori_loop(1, ncol, send_back, 0)

    send_sib(2)
    send_sib(1)
    keep_own(2)
    keep_own(1)

    def direct(i):
        j = RS - 1 - i
        xs[1, j] = summed(2, j).astype(BF16)
        last_right(j).start()
        xs[0, i] = summed(1, i).astype(BF16)
        last_left(i).start()

    loop(0, rhalf, direct)
    run(ncol, lambda d: a1(d).wait_recv())
    part2 = gws[c]
    for d in range(1, ncol):
        part2 += gwr[d]
    g2s[...] = part2
    run(nrow, lambda d: a2(d).start())

    send_sib(0)
    keep_own(0)

    def relay(i):
        j = RS - 1 - i
        first_right(i).wait_recv()
        xs[1, i] = (summed(2, i) + ra[i].astype(F32)).astype(BF16)
        last_right(i).start()
        first_left(j).wait_recv()
        xs[0, j] = (summed(1, j) + ra[j].astype(F32)).astype(BF16)
        last_left(j).start()

    loop(0, rhalf, relay)

    run(nrow, lambda d: a2(d).wait_recv())
    part3 = g2s[...]
    for d in range(1, nrow):
        part3 += g2r[d]
    gwo[c] = part3[0:wrows] * scale
    gb_out[...] = jnp.sum(part3[wrows:wrows + 8], axis=0, keepdims=True) * scale
    run(ncol, lambda d: a3(d, c).start())

    run(ncol, lambda d: back_copy(d).wait_recv())

    scan_loop(ncol, 19, lambda j: brecv[meta_s[16, j]].astype(F32))

    per = width // blk

    def gf_copy(p):
        s = pl.ds(pl.multiple_of(p * width, width), width)
        return pltpu.make_async_copy(gfv.at[s], gf_out.at[s], lsem.at[13 + p])

    def finish(p):
        total = summed(0, p)
        last_right(p).wait_recv()
        last_left(p).wait_recv()
        total = total + rb[0, p].astype(F32) + rb[1, p].astype(F32)
        for h in range(per):
            k = p * per + h
            block = total[:, h * blk:(h + 1) * blk] + scan[meta_s[18, k]]
            gfv[pl.ds(pl.multiple_of(k * blk, blk), blk), :] = block.T.astype(BF16)
        gf_copy(p).start()

    for i in range(rhalf):
        finish(i)
        finish(RS - 1 - i)

    run(ncol, lambda d: a3(d, lax.rem(c + ncol - d, ncol)).wait_recv())
    gw_out[...] = gwo[...].reshape(gw_out.shape)

    def ag_sent(p):
        own_right(p).wait_send()
        own_left(p).wait_send()
        for slot in (2, 4, 6):
            to_twin(slot, p).wait_send()
        on_right(p).wait_send()

    own_twin.wait_send()
    loop(0, AG, ag_sent)

    def rs_sent(p):
        for q in range(4):
            give(q, p).wait_send()
        first_right(p).wait_send()
        last_right(p).wait_send()
        last_left(p).wait_send()

    loop(0, RS, rs_sent)
    run(ncol, lambda d: block_copy(d).wait_send())
    run(ncol, lambda d: back_copy(d).wait_send())
    run(ncol, lambda d: a1(d).wait_send())
    run(nrow, lambda d: a2(d).wait_send())
    run(ncol, lambda d: a3(d, c).wait_send())
    hid_copy.wait()
    loop(0, RS, lambda p: gf_copy(p).wait())


def hand_over(*refs):
    sems = refs[-1]
    copies = [pltpu.make_async_copy(refs[i], refs[4 + i], sems.at[i]) for i in range(4)]
    for copy in copies:
        copy.start()
    for copy in copies:
        copy.wait()


def solution(mesh):
    nrow, ncol = mesh.shape["row"], mesh.shape["col"]

    def body(features, weight, bias_vector, stripe_values, tile_values, tile_rows, tile_slots, send_lists, cotangent):
        nodes, f = features.shape
        nt, blk, _ = tile_values.shape
        nblk = nodes // blk
        wrows = blk // ncol
        scale = 1.0 / math.sqrt(nodes * nrow * ncol)
        vm = pltpu.VMEM
        dma = pltpu.SemaphoreType.DMA
        copies = 6 * AG + 1 + 7 * RS
        any_, vmem, smem = (pl.BlockSpec(memory_space=m) for m in (pl.ANY, pltpu.VMEM, pltpu.SMEM))
        shapes = (
            jax.ShapeDtypeStruct((nodes, f), BF16),
            jax.ShapeDtypeStruct((nodes, f), BF16),
            jax.ShapeDtypeStruct((f, f), F32),
            jax.ShapeDtypeStruct((1, f), F32),
        )
        made = pl.pallas_call(
            functools.partial(kernel, nrow, ncol, scale),
            out_shape=shapes,
            in_specs=[any_, vmem, vmem, any_, any_, smem, smem, smem, any_],
            out_specs=(any_, any_, vmem, vmem),
            scratch_shapes=[
                vm((8, nodes, nodes), BF16),
                vm((nblk, blk, f), BF16),
                vm((7, nblk, blk, f), BF16),
                vm((nt, blk, blk), BF16),
                vm((nodes, f), BF16),
                vm((ncol, blk, f), BF16),
                vm((ncol, blk, f), BF16),
                vm((24, 128), jnp.int32),
                pltpu.SMEM((24, 128), jnp.int32),
                vm((nt + 1, blk, blk), F32),
                vm((nodes, f), F32),
                vm((nodes, f), BF16),
                vm((nodes, f), BF16),
                vm((nodes, f), BF16),
                vm((f, nodes), BF16),
                vm((nblk, f, blk), BF16),
                vm((4, RS, f, nodes // RS), F32),
                vm((4, RS, f, nodes // RS), BF16),
                vm((4, RS, f, nodes // RS), BF16),
                vm((3, RS, f, nodes // RS), BF16),
                vm((RS, f, nodes // RS), BF16),
                vm((2, RS, f, nodes // RS), BF16),
                vm((ncol, f, blk), BF16),
                vm((ncol, f, blk), BF16),
                vm((ncol, wrows + 8, f), F32),
                vm((ncol, wrows + 8, f), F32),
                vm((wrows + 8, f), F32),
                vm((nrow, wrows + 8, f), F32),
                vm((ncol, wrows, f), F32),
                vm((nodes, f), BF16),
                vm((8, f), F32),
                dma((13 + RS,)),
                dma((copies,)), dma((copies,)),
                dma((ncol,)), dma((ncol,)), dma((ncol,)), dma((ncol,)),
                pltpu.SemaphoreType.REGULAR,
                dma((ncol,)), dma((ncol,)), dma((nrow,)), dma((nrow,)), dma((ncol,)), dma((ncol,)),
            ],
            compiler_params=pltpu.CompilerParams(
                collective_id=0, has_side_effects=True, vmem_limit_bytes=56 * 2**20
            ),
        )(
            features.reshape(nblk, blk, f), weight, bias_vector.reshape(1, f), stripe_values, tile_values,
            tile_rows, tile_slots, send_lists.reshape(ncol), cotangent,
        )
        hid, gf, gw, gb = pl.pallas_call(
            hand_over, out_shape=shapes, in_specs=[vmem] * 4, out_specs=(any_,) * 4, scratch_shapes=[dma((4,))]
        )(*made)
        return hid, gf, gw, gb.reshape(f)

    return jax.shard_map(
        body,
        mesh=mesh,
        in_specs=(
            P(("row", "col"), None),
            P(),
            P(),
            P(("row", "col"), None),
            P(("row", "col"), None, None),
            P(("row", "col")),
            P(("row", "col")),
            P("row", "col", None, None),
            P(("row", "col"), None),
        ),
        out_specs=(P(("row", "col"), None), P(("row", "col"), None), P(), P()),
        check_vma=False,
    )
```

```python
import functools
import math

import jax
import jax.numpy as jnp
from jax import lax
from jax.experimental import pallas as pl
from jax.experimental.pallas import tpu as pltpu
from jax.sharding import PartitionSpec as P

MESH = pl.DeviceIdType.MESH
BF16 = jnp.bfloat16
F32 = jnp.float32
AG = 2
RS = 2


def mm(a, b):
    return jnp.dot(a, b, preferred_element_type=F32)


def order(read, n, lanes=128):
    sub = lax.broadcasted_iota(jnp.int32, (n, lanes), 0)
    lane = lax.broadcasted_iota(jnp.int32, (n, lanes), 1)
    col = jnp.zeros((n, lanes), jnp.int32)
    row = jnp.full((n, lanes), 1 << 20, jnp.int32)

    def one(t, both):
        v = read(t)
        return jnp.where(sub == t, v, both[0]), jnp.where(lane == t, v * n + t, both[1])

    col, row = lax.fori_loop(0, n, one, (col, row))
    less = (row < col * n + sub).astype(jnp.int32)
    rank = jnp.sum(less, axis=1, keepdims=True)
    hit = rank == lane
    perm = jnp.sum(jnp.where(hit, sub, 0), axis=0, keepdims=True)
    value = jnp.sum(jnp.where(hit, col, 0), axis=0, keepdims=True)
    last = jnp.sum((col <= lane).astype(jnp.int32), axis=0, keepdims=True)
    count = jnp.sum((col == lane).astype(jnp.int32), axis=0, keepdims=True)
    last = jnp.where(count > 0, last, 0)
    before = jnp.sum(((row // n == col) & (lane < sub)).astype(jnp.int32), axis=1, keepdims=True)
    again = jnp.sum(jnp.where(hit & (before > 0), 1, 0), axis=0, keepdims=True)
    return jnp.concatenate([perm, value, last, again] + [jnp.zeros_like(perm)] * 4, axis=0)


def kernel(
    nrow, ncol, scale,
    feat, weight, bias, stripe, tiles, rows_s, slots_s, lists_s, cot,
    hid_out, gf_out, gw_out, gb_out,
    st, fo, fg, tv, cv, recv, stage, meta_v, meta_s, scan, y, yb, gp, hid, gt, gtb,
    pa, ps, sr, xs, ra, rb, bst, brecv, gws, gwr, g2s, g2r, gwo, gfv, biasp,
    lsem, rsem, fsem, frsem, bsem, brsem, gsem, tsem, heard, a1s, a1r, a2s, a2r, a3s, a3r,
):
    nblk, blk, _ = feat.shape
    nt = tv.shape[0]
    nodes = nblk * blk
    r = lax.axis_index("row")
    c = lax.axis_index("col")
    chip, core = r // 2, r % 2
    chips = nrow // 2
    chip_r, chip_l, chip_f = (chip + 1) % chips, (chip + chips - 1) % chips, (chip + 2) % chips
    sib = chip * 2 + 1 - core
    right, left = chip_r * 2 + core, chip_l * 2 + core
    order_of = [
        chip * 2 + core, chip * 2 + 1 - core,
        chip_l * 2 + core, chip_l * 2 + 1 - core,
        chip_r * 2 + core, chip_r * 2 + 1 - core,
        chip_f * 2 + core, chip_f * 2 + 1 - core,
    ]

    side = next(k for k in range(1, ncol + 1) if k * k >= ncol)
    lines = ncol // side
    cy, cz = c // side, c % side

    def peer(d):
        return lax.rem(cy + d // side, lines) * side + lax.rem(cz + d % side, side)

    def back_peer(d):
        return lax.rem(cy + lines - d // side, lines) * side + lax.rem(cz + side - d % side, side)

    def offset(q):
        return lax.rem(cy + lines - q // side, lines) * side + lax.rem(cz + side - q % side, side)

    local = [
        pltpu.make_async_copy(feat, fo, lsem.at[8]),
        pltpu.make_async_copy(cot, cv, lsem.at[9]),
        pltpu.make_async_copy(tiles, tv, lsem.at[10]),
    ]
    local[0].start()
    stripes = [
        pltpu.make_async_copy(
            stripe.at[:, pl.ds(pl.multiple_of(order_of[k] * nodes, 128), nodes)], st.at[k], lsem.at[k]
        )
        for k in range(8)
    ]
    stripes[0].start()
    stripes[1].start()
    for k in range(2, 8):
        stripes[k].start()
    local[2].start()
    local[1].start()
    barrier = pltpu.get_barrier_semaphore()

    others = [(row, c) for row in (sib, right, left)]
    z_peers = [(r, cy * side + (cz + d) % side) for d in range(1, side)]
    y_peers = [(r, (cy + d) % lines * side + cz) for d in range(1, lines)]
    for dev in others + z_peers + y_peers:
        pl.semaphore_signal(barrier, inc=1, device_id=dev, device_id_type=MESH)

    meta_v[0:8] = order(lambda t: rows_s[t], nt)
    meta_v[8:16] = order(lambda t: offset(slots_s[t]), nt)
    meta_v[16:24] = order(lambda d: lists_s[peer(d)], ncol)
    meta_copy = pltpu.make_async_copy(meta_v, meta_s, lsem.at[11])
    meta_copy.start()

    pl.semaphore_wait(barrier, len(others + z_peers + y_peers))
    for dev in z_peers:
        pl.semaphore_signal(heard, inc=1, device_id=dev, device_id_type=MESH)

    piece, half = nodes // AG, AG // 2
    pb = piece // blk
    width, rhalf = nodes // RS, RS // 2

    def remote(i, src, dst, row, sent=gsem):
        return pltpu.make_async_remote_copy(
            src_ref=src, dst_ref=dst, send_sem=sent, recv_sem=rsem.at[i],
            device_id=(row, c), device_id_type=MESH,
        )

    def whole(ref, sent, received):
        return pltpu.make_async_remote_copy(
            src_ref=ref, dst_ref=ref, send_sem=sent, recv_sem=received,
            device_id=(sib, c), device_id_type=MESH,
        )

    def after_first(ref, sent, received):
        return whole(ref.at[pl.ds(1, ref.shape[0] - 1)], sent, received)

    def part(slot, p):
        own = fo if slot == 0 else fg.at[slot - 1]
        return own.at[pl.ds(p * pb, pb)]

    def own_right(p):
        return remote(p, part(0, p), part(2, p), right)

    def own_left(p):
        return remote(AG + p, part(0, p), part(4, p), left)

    def on_right(p):
        return remote(2 * AG + p, part(2, p), part(6, p), right)

    def on_left(p):
        return remote(2 * AG + p, part(4, p), part(6, p), left)

    def to_twin(slot, p):
        return remote(3 * AG + (slot - 2) // 2 * AG + p, part(slot, p), part(slot + 1, p), sib)

    own_twin = remote(6 * AG, fo, fg.at[0], sib)
    base = 6 * AG + 1

    def give(q, p):
        return remote(base + q * RS + p, ps.at[q, p], sr.at[q, p], sib, tsem)

    def first_right(p):
        return remote(base + 4 * RS + p, xs.at[2, p], ra.at[p], right, tsem)

    def first_left(p):
        return remote(base + 4 * RS + p, xs.at[2, p], ra.at[p], left, tsem)

    def last_right(p):
        return remote(base + 5 * RS + p, xs.at[1, p], rb.at[1, p], right, tsem)

    def last_left(p):
        return remote(base + 6 * RS + p, xs.at[0, p], rb.at[0, p], left, tsem)

    def loop(start, stop, act):
        def one(d, _):
            act(d)
            return 0

        lax.fori_loop(start, stop, one, 0)

    local[0].wait()
    own_right(0).start()
    own_left(AG - 1).start()
    own_twin.start()

    def own(i):
        own_right(i).start()
        own_left(AG - 1 - i).start()

    loop(1, AG, own)
    def block_copy(d):
        return pltpu.make_async_remote_copy(
            src_ref=stage.at[d], dst_ref=recv.at[d], send_sem=fsem, recv_sem=frsem,
            device_id=(r, peer(d)), device_id_type=MESH,
        )

    def picked(d):
        return fo[lists_s[peer(d)]]

    def send_block(d):
        stage[d] = picked(d)
        block_copy(d).start()

    def send_blocks():
        pl.semaphore_wait(heard, len(z_peers))
        for i in range(1, lines):
            loop(i * side + 1, (i + 1) * side, send_block)

    loop(1, side, send_block)
    loop(1, lines, lambda i: send_block(i * side))
    recv[0] = picked(0)

    def dense_all(slot, fresh):
        rows = nodes // 2
        src = fo if slot == 0 else fg.at[slot - 1]

        def one(i):
            at = pl.ds(pl.multiple_of(i * rows, rows), rows)
            v = mm(st[slot, at, :], src[...].reshape(nodes, -1))
            y[at, :] = v if fresh else y[at, :] + v

        loop(0, 2, one)

    stripes[0].wait()
    dense_all(0, True)
    stripes[1].wait()
    own_twin.wait_recv()
    dense_all(1, False)
    scan[0] = jnp.zeros((blk, blk), F32)

    def same(row, j):
        return meta_s[row, j].astype(F32)

    unroll = 4

    def scan_loop(n, row, term):
        def step(i):
            terms = [term(i * unroll + u) for u in range(unroll)]
            run_sum = scan[i * unroll]
            for u in range(unroll):
                run_sum = terms[u] + same(row, i * unroll + u) * run_sum
                scan[i * unroll + u + 1] = run_sum

        loop(0, n // unroll, step)

    def sparse_forward():
        meta_copy.wait()
        local[2].wait()
        after_first(recv, fsem, frsem).wait_recv()

        def product(j):
            t = meta_s[0, j]
            return mm(tv[t], recv[offset(slots_s[t])])

        scan_loop(nt, 3, product)

        def put(k):
            y[pl.ds(pl.multiple_of(k * blk, blk), blk), :] += scan[meta_s[2, k]]

        loop(0, nblk, put)

    def add(one, p, two, q):
        rows = nodes // 2

        def half_rows(i):
            at = pl.ds(pl.multiple_of(i * rows, rows), rows)
            parts = [
                mm(st[slot, at, u * piece:(u + 1) * piece], fg[slot - 1, u * pb:(u + 1) * pb].reshape(piece, -1))
                for slot, u in ((one, p), (two, q))
            ]
            y[at, :] += parts[0] + parts[1]

        loop(0, 2, half_rows)

    def arrive(i):
        j = AG - 1 - i
        own_right(i).wait_recv()
        if i < half:
            on_right(i).start()
        to_twin(2, i).start()
        own_left(j).wait_recv()
        if i < half:
            on_left(j).start()
        to_twin(4, j).start()

    def twins(i):
        j = AG - 1 - i
        to_twin(2, i).wait_recv()
        to_twin(4, j).wait_recv()
        add(3, i, 5, j)

    def arrive_far(i):
        j = AG - 1 - i
        on_right(i).wait_recv()
        to_twin(6, i).start()
        on_left(j).wait_recv()
        to_twin(6, j).start()

    def far_twins(i):
        j = AG - 1 - i
        to_twin(6, i).wait_recv()
        to_twin(6, j).wait_recv()
        add(7, i, 7, j)

    for i in range(AG):
        arrive(i)
        if i == 0:
            send_blocks()
            stripes[2].wait()
            stripes[4].wait()
        add(2, i, 4, AG - 1 - i)
        if i == 0:
            stripes[3].wait()
            stripes[5].wait()
        else:
            twins(i - 1)
    twins(AG - 1)
    stripes[6].wait()
    stripes[7].wait()
    for i in range(half):
        arrive_far(i)
        add(6, i, 6, AG - 1 - i)
        if i == 0:
            sparse_forward()
        else:
            far_twins(i - 1)
    far_twins(half - 1)

    local[1].wait()
    w = weight[...]
    chunk = 4 * blk
    biasp[...] = jnp.zeros_like(biasp)

    def pointwise(k):
        s = pl.ds(pl.multiple_of(k * chunk, chunk), chunk)
        yk = y[s, :].astype(BF16)
        yb[s, :] = yk
        x = mm(yk, w) + bias[...]
        g = jax.nn.sigmoid(x)
        hid[s, :] = (x * g).astype(BF16)
        gk = (cv[s, :].astype(F32) * (g * (1.0 + x * (1.0 - g)))).astype(BF16)
        gp[s, :] = gk
        biasp[...] += jnp.sum(gk.astype(F32).reshape(chunk // 8, 8, blk), axis=0)
        gtk = lax.dot_general(w, gk, (((1,), (1,)), ((), ())), preferred_element_type=F32).astype(BF16)
        gt[:, s] = gtk
        for h in range(4):
            gtb[4 * k + h] = gtk[:, h * blk:(h + 1) * blk]

    loop(0, nodes // chunk, pointwise)
    hid_copy = pltpu.make_async_copy(hid, hid_out, lsem.at[12])
    hid_copy.start()

    group = min(2, RS)

    def back(slot, i):
        wide = group * width
        return mm(gt[...], st[slot, :, pl.ds(pl.multiple_of(i * wide, wide), wide)])

    def send_sib(q):
        def one(i):
            v = back(2 * q + 1, i).astype(BF16)
            for u in range(group):
                ps[q, i * group + u] = v[:, u * width:(u + 1) * width]
                give(q, i * group + u).start()

        loop(0, RS // group, one)

    def keep_own(q):
        def one(i):
            v = back(2 * q, i)
            for u in range(group):
                pa[q, i * group + u] = v[:, u * width:(u + 1) * width]

        loop(0, RS // group, one)

    def summed(q, p):
        give(q, p).wait_recv()
        return pa[q, p] + sr[q, p].astype(F32)

    send_sib(3)

    gw = lax.dot_general(yb[...], gp[...], (((0,), (0,)), ((), ())), preferred_element_type=F32)
    wrows = blk // ncol
    for q in range(ncol):
        gws[q, 0:wrows] = gw[q * wrows:(q + 1) * wrows, :]
        gws[q, wrows:wrows + 8] = biasp[...]

    def a1(d):
        return pltpu.make_async_remote_copy(
            src_ref=gws.at[peer(d)], dst_ref=gwr.at[d], send_sem=a1s, recv_sem=a1r,
            device_id=(r, peer(d)), device_id_type=MESH,
        )

    def a2(d):
        return pltpu.make_async_remote_copy(
            src_ref=g2s, dst_ref=g2r.at[d], send_sem=a2s, recv_sem=a2r,
            device_id=(lax.rem(r + d, nrow), c), device_id_type=MESH,
        )

    def a3(d):
        return pltpu.make_async_remote_copy(
            src_ref=gwo.at[0], dst_ref=gwo.at[d], send_sem=a3s, recv_sem=a3r,
            device_id=(r, peer(d)), device_id_type=MESH,
        )

    def run(n, act):
        loop(1, n, act)

    run(ncol, lambda d: a1(d).start())

    keep_own(3)

    def first(i):
        j = RS - 1 - i
        xs[2, i] = summed(3, i).astype(BF16)
        first_right(i).start()
        xs[2, j] = summed(3, j).astype(BF16)
        first_left(j).start()

    loop(0, rhalf, first)

    def back_copy(d):
        return pltpu.make_async_remote_copy(
            src_ref=bst.at[d], dst_ref=brecv.at[d], send_sem=bsem, recv_sem=brsem,
            device_id=(r, back_peer(d)), device_id_type=MESH,
        )

    def bproduct(j):
        t = meta_s[8, j]
        return mm(gtb[rows_s[t]], tv[t])

    scan_loop(nt, 11, bproduct)

    def slot_sum(d):
        return scan[meta_s[10, d]].astype(BF16)

    brecv[0] = slot_sum(0)

    def send_back(d, _):
        bst[d] = slot_sum(d)
        back_copy(d).start()
        return 0

    lax.fori_loop(1, ncol, send_back, 0)

    send_sib(2)
    send_sib(1)
    keep_own(2)
    keep_own(1)
    after_first(gwr, a1s, a1r).wait_recv()
    part2 = gws[c]
    for d in range(1, ncol):
        part2 += gwr[d]
    g2s[...] = part2
    run(nrow, lambda d: a2(d).start())


    def direct(i):
        j = RS - 1 - i
        xs[1, j] = summed(2, j).astype(BF16)
        last_right(j).start()
        xs[0, i] = summed(1, i).astype(BF16)
        last_left(i).start()

    loop(0, rhalf, direct)
    send_sib(0)
    keep_own(0)

    def relay(i):
        j = RS - 1 - i
        first_right(i).wait_recv()
        xs[1, i] = (summed(2, i) + ra[i].astype(F32)).astype(BF16)
        last_right(i).start()
        first_left(j).wait_recv()
        xs[0, j] = (summed(1, j) + ra[j].astype(F32)).astype(BF16)
        last_left(j).start()

    whole(fg, gsem, gsem).wait_send()
    after_first(stage, fsem, frsem).wait_send()
    loop(0, rhalf, relay)

    after_first(g2r, a2s, a2r).wait_recv()
    part3 = g2s[...]
    for d in range(1, nrow):
        part3 += g2r[d]
    gwo[0] = part3[0:wrows] * scale
    gb_out[...] = jnp.sum(part3[wrows:wrows + 8], axis=0, keepdims=True) * scale
    run(ncol, lambda d: a3(d).start())

    after_first(brecv, bsem, brsem).wait_recv()

    scan_loop(ncol, 19, lambda j: brecv[meta_s[16, j]].astype(F32))

    per = width // blk

    def gf_copy(p):
        s = pl.ds(pl.multiple_of(p * width, width), width)
        return pltpu.make_async_copy(gfv.at[s], gf_out.at[s], lsem.at[13 + p])

    def prepare(p, direct, from_side):
        total = summed(0, p)
        direct(p).wait_recv()
        pa[0, p] = total + rb[from_side, p].astype(F32)

    def finish(p, relayed, from_side):
        relayed(p).wait_recv()
        total = pa[0, p] + rb[from_side, p].astype(F32)
        for h in range(per):
            k = p * per + h
            block = total[:, h * blk:(h + 1) * blk] + scan[meta_s[18, k]]
            gfv[pl.ds(pl.multiple_of(k * blk, blk), blk), :] = block.T.astype(BF16)
        gf_copy(p).start()

    for i in range(rhalf):
        prepare(i, last_left, 0)
        prepare(RS - 1 - i, last_right, 1)
    after_first(bst, bsem, brsem).wait_send()
    after_first(gwr, a1s, a1r).wait_send()
    after_first(g2r, a2s, a2r).wait_send()
    for i in range(rhalf):
        finish(i, last_right, 1)
        finish(RS - 1 - i, last_left, 0)

    after_first(gwo, a3s, a3r).wait_recv()

    def place(d):
        at = pl.multiple_of(back_peer(d) * wrows, wrows)
        gw_out[pl.ds(at, wrows), :] = gwo[d]

    loop(0, ncol, place)
    after_first(gwo, a3s, a3r).wait_send()
    whole(fg, tsem, tsem).wait_send()
    hid_copy.wait()
    loop(0, RS, lambda p: gf_copy(p).wait())


def hand_over(*refs):
    sems = refs[-1]
    copies = [pltpu.make_async_copy(refs[i], refs[4 + i], sems.at[i]) for i in range(4)]
    for copy in copies:
        copy.start()
    for copy in copies:
        copy.wait()


def solution(mesh):
    nrow, ncol = mesh.shape["row"], mesh.shape["col"]

    def body(features, weight, bias_vector, stripe_values, tile_values, tile_rows, tile_slots, send_lists, cotangent):
        nodes, f = features.shape
        nt, blk, _ = tile_values.shape
        nblk = nodes // blk
        wrows = blk // ncol
        scale = 1.0 / math.sqrt(nodes * nrow * ncol)
        vm = pltpu.VMEM
        dma = pltpu.SemaphoreType.DMA
        copies = 6 * AG + 1 + 7 * RS
        any_, vmem, smem = (pl.BlockSpec(memory_space=m) for m in (pl.ANY, pltpu.VMEM, pltpu.SMEM))
        shapes = (
            jax.ShapeDtypeStruct((nodes, f), BF16),
            jax.ShapeDtypeStruct((nodes, f), BF16),
            jax.ShapeDtypeStruct((f, f), F32),
            jax.ShapeDtypeStruct((1, f), F32),
        )
        made = pl.pallas_call(
            functools.partial(kernel, nrow, ncol, scale),
            out_shape=shapes,
            in_specs=[any_, vmem, vmem, any_, any_, smem, smem, smem, any_],
            out_specs=(any_, any_, vmem, vmem),
            scratch_shapes=[
                vm((8, nodes, nodes), BF16),
                vm((nblk, blk, f), BF16),
                vm((7, nblk, blk, f), BF16),
                vm((nt, blk, blk), BF16),
                vm((nodes, f), BF16),
                vm((ncol, blk, f), BF16),
                vm((ncol, blk, f), BF16),
                vm((24, 128), jnp.int32),
                pltpu.SMEM((24, 128), jnp.int32),
                vm((nt + 1, blk, blk), F32),
                vm((nodes, f), F32),
                vm((nodes, f), BF16),
                vm((nodes, f), BF16),
                vm((nodes, f), BF16),
                vm((f, nodes), BF16),
                vm((nblk, f, blk), BF16),
                vm((4, RS, f, nodes // RS), F32),
                vm((4, RS, f, nodes // RS), BF16),
                vm((4, RS, f, nodes // RS), BF16),
                vm((3, RS, f, nodes // RS), BF16),
                vm((RS, f, nodes // RS), BF16),
                vm((2, RS, f, nodes // RS), BF16),
                vm((ncol, f, blk), BF16),
                vm((ncol, f, blk), BF16),
                vm((ncol, wrows + 8, f), F32),
                vm((ncol, wrows + 8, f), F32),
                vm((wrows + 8, f), F32),
                vm((nrow, wrows + 8, f), F32),
                vm((ncol, wrows, f), F32),
                vm((nodes, f), BF16),
                vm((8, f), F32),
                dma((13 + RS,)),
                dma((copies,)),
                dma(()), dma(()), dma(()), dma(()), dma(()), dma(()),
                pltpu.SemaphoreType.REGULAR,
                dma(()), dma(()), dma(()), dma(()), dma(()), dma(()),
            ],
            compiler_params=pltpu.CompilerParams(
                collective_id=0, has_side_effects=True, vmem_limit_bytes=56 * 2**20
            ),
        )(
            features.reshape(nblk, blk, f), weight, bias_vector.reshape(1, f), stripe_values, tile_values,
            tile_rows, tile_slots, send_lists.reshape(ncol), cotangent,
        )
        hid, gf, gw, gb = pl.pallas_call(
            hand_over, out_shape=shapes, in_specs=[vmem] * 4, out_specs=(any_,) * 4, scratch_shapes=[dma((4,))]
        )(*made)
        return hid, gf, gw, gb.reshape(f)

    return jax.shard_map(
        body,
        mesh=mesh,
        in_specs=(
            P(("row", "col"), None),
            P(),
            P(),
            P(("row", "col"), None),
            P(("row", "col"), None, None),
            P(("row", "col")),
            P(("row", "col")),
            P("row", "col", None, None),
            P(("row", "col"), None),
        ),
        out_specs=(P(("row", "col"), None), P(("row", "col"), None), P(), P()),
        check_vma=False,
    )
```

```python
import functools
import math

import jax
import jax.numpy as jnp
from jax import lax
from jax.experimental import pallas as pl
from jax.experimental.pallas import tpu as pltpu
from jax.sharding import PartitionSpec as P

MESH = pl.DeviceIdType.MESH
BF16 = jnp.bfloat16
F32 = jnp.float32
AG = 2
RS = 2


def mm(a, b):
    return jnp.dot(a, b, preferred_element_type=F32)


def order(read, n, lanes=128):
    sub = lax.broadcasted_iota(jnp.int32, (n, lanes), 0)
    lane = lax.broadcasted_iota(jnp.int32, (n, lanes), 1)
    col = jnp.zeros((n, lanes), jnp.int32)
    row = jnp.full((n, lanes), 1 << 20, jnp.int32)

    def one(t, both):
        v = read(t)
        return jnp.where(sub == t, v, both[0]), jnp.where(lane == t, v * n + t, both[1])

    col, row = lax.fori_loop(0, n, one, (col, row))
    less = (row < col * n + sub).astype(jnp.int32)
    rank = jnp.sum(less, axis=1, keepdims=True)
    hit = rank == lane
    perm = jnp.sum(jnp.where(hit, sub, 0), axis=0, keepdims=True)
    value = jnp.sum(jnp.where(hit, col, 0), axis=0, keepdims=True)
    last = jnp.sum((col <= lane).astype(jnp.int32), axis=0, keepdims=True)
    count = jnp.sum((col == lane).astype(jnp.int32), axis=0, keepdims=True)
    last = jnp.where(count > 0, last, 0)
    before = jnp.sum(((row // n == col) & (lane < sub)).astype(jnp.int32), axis=1, keepdims=True)
    again = jnp.sum(jnp.where(hit & (before > 0), 1, 0), axis=0, keepdims=True)
    return jnp.concatenate([perm, value, last, again] + [jnp.zeros_like(perm)] * 4, axis=0)


def kernel(
    nrow, ncol, scale,
    feat, weight_h, bias_h, stripe, tiles, rows_h, slots_h, lists_h, cot,
    hid_out, gf_out, gw_out, gb_out,
    weight, bias, rows_s, slots_s, lists_s, st, fo, fg, tv, cv, recv, stage, meta_v, meta_s, scan, y, yb, gp, hid, gt, gtb,
    pa, ps, sr, xs, ra, rb, bst, brecv, gws, gwr, g2s, g2r, gwo, gfv, biasp,
    lsem, rsem, fsem, frsem, bsem, brsem, gsem, tsem, heard, a1s, a1r, a2s, a2r, a3s, a3r,
):
    nblk, blk, _ = feat.shape
    nt = tv.shape[0]
    nodes = nblk * blk
    small = [
        pltpu.make_async_copy(x, y_, lsem.at[13 + RS + i])
        for i, (x, y_) in enumerate(
            [(rows_h, rows_s), (slots_h, slots_s), (lists_h, lists_s), (weight_h, weight), (bias_h, bias)]
        )
    ]
    r = lax.axis_index("row")
    c = lax.axis_index("col")
    chip, core = r // 2, r % 2
    chips = nrow // 2
    chip_r, chip_l, chip_f = (chip + 1) % chips, (chip + chips - 1) % chips, (chip + 2) % chips
    sib = chip * 2 + 1 - core
    right, left = chip_r * 2 + core, chip_l * 2 + core
    order_of = [
        chip * 2 + core, chip * 2 + 1 - core,
        chip_l * 2 + core, chip_l * 2 + 1 - core,
        chip_r * 2 + core, chip_r * 2 + 1 - core,
        chip_f * 2 + core, chip_f * 2 + 1 - core,
    ]

    side = next(k for k in range(1, ncol + 1) if k * k >= ncol)
    lines = ncol // side
    cy, cz = c // side, c % side

    def peer(d):
        return lax.rem(cy + d // side, lines) * side + lax.rem(cz + d % side, side)

    def back_peer(d):
        return lax.rem(cy + lines - d // side, lines) * side + lax.rem(cz + side - d % side, side)

    def offset(q):
        return lax.rem(cy + lines - q // side, lines) * side + lax.rem(cz + side - q % side, side)

    local = [
        pltpu.make_async_copy(feat, fo, lsem.at[8]),
        pltpu.make_async_copy(cot, cv, lsem.at[9]),
        pltpu.make_async_copy(tiles, tv, lsem.at[10]),
    ]
    barrier = pltpu.get_barrier_semaphore()

    others = [(row, c) for row in (sib, right, left)]
    z_peers = [(r, cy * side + (cz + d) % side) for d in range(1, side)]
    y_peers = [(r, (cy + d) % lines * side + cz) for d in range(1, lines)]
    for dev in others + z_peers + y_peers:
        pl.semaphore_signal(barrier, inc=1, device_id=dev, device_id_type=MESH)

    for copy in small:
        copy.start()
    local[0].start()
    stripes = [
        pltpu.make_async_copy(
            stripe.at[:, pl.ds(pl.multiple_of(order_of[k] * nodes, 128), nodes)], st.at[k], lsem.at[k]
        )
        for k in range(8)
    ]
    stripes[0].start()
    stripes[1].start()
    for k in range(2, 8):
        stripes[k].start()
    local[2].start()
    local[1].start()
    for copy in small:
        copy.wait()
    meta_v[0:8] = order(lambda t: rows_s[t], nt)
    meta_v[8:16] = order(lambda t: offset(slots_s[t]), nt)
    meta_v[16:24] = order(lambda d: lists_s[peer(d)], ncol)
    meta_copy = pltpu.make_async_copy(meta_v, meta_s, lsem.at[11])
    meta_copy.start()

    pl.semaphore_wait(barrier, len(others + z_peers + y_peers))
    for dev in z_peers:
        pl.semaphore_signal(heard, inc=1, device_id=dev, device_id_type=MESH)

    piece, half = nodes // AG, AG // 2
    pb = piece // blk
    width, rhalf = nodes // RS, RS // 2

    def remote(i, src, dst, row, sent=gsem):
        return pltpu.make_async_remote_copy(
            src_ref=src, dst_ref=dst, send_sem=sent, recv_sem=rsem.at[i],
            device_id=(row, c), device_id_type=MESH,
        )

    def whole(ref, sent, received):
        return pltpu.make_async_remote_copy(
            src_ref=ref, dst_ref=ref, send_sem=sent, recv_sem=received,
            device_id=(sib, c), device_id_type=MESH,
        )

    def after_first(ref, sent, received):
        return whole(ref.at[pl.ds(1, ref.shape[0] - 1)], sent, received)

    def part(slot, p):
        own = fo if slot == 0 else fg.at[slot - 1]
        return own.at[pl.ds(p * pb, pb)]

    def own_right(p):
        return remote(p, part(0, p), part(2, p), right)

    def own_left(p):
        return remote(AG + p, part(0, p), part(4, p), left)

    def on_right(p):
        return remote(2 * AG + p, part(2, p), part(6, p), right)

    def on_left(p):
        return remote(2 * AG + p, part(4, p), part(6, p), left)

    def to_twin(slot, p):
        return remote(3 * AG + (slot - 2) // 2 * AG + p, part(slot, p), part(slot + 1, p), sib)

    own_twin = remote(6 * AG, fo, fg.at[0], sib)
    base = 6 * AG + 1

    def give(q, p):
        return remote(base + q * RS + p, ps.at[q, p], sr.at[q, p], sib, tsem)

    def first_right(p):
        return remote(base + 4 * RS + p, xs.at[2, p], ra.at[p], right, tsem)

    def first_left(p):
        return remote(base + 4 * RS + p, xs.at[2, p], ra.at[p], left, tsem)

    def last_right(p):
        return remote(base + 5 * RS + p, xs.at[1, p], rb.at[1, p], right, tsem)

    def last_left(p):
        return remote(base + 6 * RS + p, xs.at[0, p], rb.at[0, p], left, tsem)

    def loop(start, stop, act):
        def one(d, _):
            act(d)
            return 0

        lax.fori_loop(start, stop, one, 0)

    local[0].wait()
    own_right(0).start()
    own_left(AG - 1).start()
    own_twin.start()

    def own(i):
        own_right(i).start()
        own_left(AG - 1 - i).start()

    loop(1, AG, own)
    def block_copy(d):
        return pltpu.make_async_remote_copy(
            src_ref=stage.at[d], dst_ref=recv.at[d], send_sem=fsem, recv_sem=frsem,
            device_id=(r, peer(d)), device_id_type=MESH,
        )

    def picked(d):
        return fo[lists_s[peer(d)]]

    def send_block(d):
        stage[d] = picked(d)
        block_copy(d).start()

    def send_blocks():
        pl.semaphore_wait(heard, len(z_peers))
        for i in range(1, lines):
            loop(i * side + 1, (i + 1) * side, send_block)

    loop(1, side, send_block)
    loop(1, lines, lambda i: send_block(i * side))
    recv[0] = picked(0)

    def dense_all(slot, fresh):
        rows = nodes // 2
        src = fo if slot == 0 else fg.at[slot - 1]

        def one(i):
            at = pl.ds(pl.multiple_of(i * rows, rows), rows)
            v = mm(st[slot, at, :], src[...].reshape(nodes, -1))
            y[at, :] = v if fresh else y[at, :] + v

        loop(0, 2, one)

    stripes[0].wait()
    dense_all(0, True)
    stripes[1].wait()
    own_twin.wait_recv()
    dense_all(1, False)
    scan[0] = jnp.zeros((blk, blk), F32)

    def same(row, j):
        return meta_s[row, j].astype(F32)

    unroll = 4

    def scan_loop(n, row, term):
        def step(i):
            terms = [term(i * unroll + u) for u in range(unroll)]
            run_sum = scan[i * unroll]
            for u in range(unroll):
                run_sum = terms[u] + same(row, i * unroll + u) * run_sum
                scan[i * unroll + u + 1] = run_sum

        loop(0, n // unroll, step)

    def sparse_forward():
        meta_copy.wait()
        local[2].wait()
        after_first(recv, fsem, frsem).wait_recv()

        def product(j):
            t = meta_s[0, j]
            return mm(tv[t], recv[offset(slots_s[t])])

        scan_loop(nt, 3, product)

        def put(k):
            y[pl.ds(pl.multiple_of(k * blk, blk), blk), :] += scan[meta_s[2, k]]

        loop(0, nblk, put)

    def add(one, p, two, q):
        rows = nodes // 2

        def half_rows(i):
            at = pl.ds(pl.multiple_of(i * rows, rows), rows)
            parts = [
                mm(st[slot, at, u * piece:(u + 1) * piece], fg[slot - 1, u * pb:(u + 1) * pb].reshape(piece, -1))
                for slot, u in ((one, p), (two, q))
            ]
            y[at, :] += parts[0] + parts[1]

        loop(0, 2, half_rows)

    def arrive(i):
        j = AG - 1 - i
        own_right(i).wait_recv()
        if i < half:
            on_right(i).start()
        to_twin(2, i).start()
        own_left(j).wait_recv()
        if i < half:
            on_left(j).start()
        to_twin(4, j).start()

    def twins(i):
        j = AG - 1 - i
        to_twin(2, i).wait_recv()
        to_twin(4, j).wait_recv()
        add(3, i, 5, j)

    def arrive_far(i):
        j = AG - 1 - i
        on_right(i).wait_recv()
        to_twin(6, i).start()
        on_left(j).wait_recv()
        to_twin(6, j).start()

    def far_twins(i):
        j = AG - 1 - i
        to_twin(6, i).wait_recv()
        to_twin(6, j).wait_recv()
        add(7, i, 7, j)

    send_blocks()
    for i in range(AG):
        arrive(i)
        if i == 0:
            stripes[2].wait()
            stripes[4].wait()
        add(2, i, 4, AG - 1 - i)
        if i == 0:
            stripes[3].wait()
            stripes[5].wait()
        else:
            twins(i - 1)
    twins(AG - 1)
    stripes[6].wait()
    stripes[7].wait()
    for i in range(half):
        arrive_far(i)
        add(6, i, 6, AG - 1 - i)
        if i == 0:
            sparse_forward()
        else:
            far_twins(i - 1)
    far_twins(half - 1)

    local[1].wait()
    w = weight[...]
    chunk = 8 * blk
    biasp[...] = jnp.zeros_like(biasp)

    def pointwise(k):
        s = pl.ds(pl.multiple_of(k * chunk, chunk), chunk)
        yk = y[s, :].astype(BF16)
        yb[s, :] = yk
        x = mm(yk, w) + bias[...]
        g = jax.nn.sigmoid(x)
        hid[s, :] = (x * g).astype(BF16)
        gk = (cv[s, :].astype(F32) * (g * (1.0 + x * (1.0 - g)))).astype(BF16)
        gp[s, :] = gk
        biasp[...] += jnp.sum(gk.astype(F32).reshape(chunk // 8, 8, blk), axis=0)
        gtk = lax.dot_general(w, gk, (((1,), (1,)), ((), ())), preferred_element_type=F32).astype(BF16)
        gt[:, s] = gtk
        for h in range(8):
            gtb[8 * k + h] = gtk[:, h * blk:(h + 1) * blk]

    loop(0, nodes // chunk, pointwise)
    hid_copy = pltpu.make_async_copy(hid, hid_out, lsem.at[12])
    hid_copy.start()

    group = min(2, RS)

    def back(slot, i):
        wide = group * width
        return mm(gt[...], st[slot, :, pl.ds(pl.multiple_of(i * wide, wide), wide)])

    def send_sib(q):
        def one(i):
            v = back(2 * q + 1, i).astype(BF16)
            for u in range(group):
                ps[q, i * group + u] = v[:, u * width:(u + 1) * width]
                give(q, i * group + u).start()

        loop(0, RS // group, one)

    def keep_own(q):
        def one(i):
            v = back(2 * q, i)
            for u in range(group):
                pa[q, i * group + u] = v[:, u * width:(u + 1) * width]

        loop(0, RS // group, one)

    def summed(q, p):
        give(q, p).wait_recv()
        return pa[q, p] + sr[q, p].astype(F32)

    send_sib(3)

    gw = lax.dot_general(yb[...], gp[...], (((0,), (0,)), ((), ())), preferred_element_type=F32)
    wrows = blk // ncol
    for q in range(ncol):
        gws[q, 0:wrows] = gw[q * wrows:(q + 1) * wrows, :]
        gws[q, wrows:wrows + 8] = biasp[...]

    def a1(d):
        return pltpu.make_async_remote_copy(
            src_ref=gws.at[peer(d)], dst_ref=gwr.at[d], send_sem=a1s, recv_sem=a1r,
            device_id=(r, peer(d)), device_id_type=MESH,
        )

    def a2(d):
        return pltpu.make_async_remote_copy(
            src_ref=g2s, dst_ref=g2r.at[d], send_sem=a2s, recv_sem=a2r,
            device_id=(lax.rem(r + d, nrow), c), device_id_type=MESH,
        )

    def a3(d):
        return pltpu.make_async_remote_copy(
            src_ref=gwo.at[0], dst_ref=gwo.at[d], send_sem=a3s, recv_sem=a3r,
            device_id=(r, peer(d)), device_id_type=MESH,
        )

    def run(n, act):
        loop(1, n, act)

    run(ncol, lambda d: a1(d).start())

    keep_own(3)

    def first(i):
        j = RS - 1 - i
        xs[2, i] = summed(3, i).astype(BF16)
        first_right(i).start()
        xs[2, j] = summed(3, j).astype(BF16)
        first_left(j).start()

    loop(0, rhalf, first)

    def back_copy(d):
        return pltpu.make_async_remote_copy(
            src_ref=bst.at[d], dst_ref=brecv.at[d], send_sem=bsem, recv_sem=brsem,
            device_id=(r, back_peer(d)), device_id_type=MESH,
        )

    def bproduct(j):
        t = meta_s[8, j]
        return mm(gtb[rows_s[t]], tv[t])

    scan_loop(nt, 11, bproduct)

    def slot_sum(d):
        return scan[meta_s[10, d]].astype(BF16)

    brecv[0] = slot_sum(0)

    def send_back(d, _):
        bst[d] = slot_sum(d)
        back_copy(d).start()
        return 0

    lax.fori_loop(1, ncol, send_back, 0)

    send_sib(2)
    send_sib(1)
    keep_own(2)
    keep_own(1)
    after_first(gwr, a1s, a1r).wait_recv()
    part2 = gws[c]
    for d in range(1, ncol):
        part2 += gwr[d]
    g2s[...] = part2
    run(nrow, lambda d: a2(d).start())


    def direct(i):
        j = RS - 1 - i
        xs[1, j] = summed(2, j).astype(BF16)
        last_right(j).start()
        xs[0, i] = summed(1, i).astype(BF16)
        last_left(i).start()

    loop(0, rhalf, direct)
    send_sib(0)
    keep_own(0)

    def relay(i):
        j = RS - 1 - i
        first_right(i).wait_recv()
        xs[1, i] = (summed(2, i) + ra[i].astype(F32)).astype(BF16)
        last_right(i).start()
        first_left(j).wait_recv()
        xs[0, j] = (summed(1, j) + ra[j].astype(F32)).astype(BF16)
        last_left(j).start()

    whole(fg, gsem, gsem).wait_send()
    after_first(stage, fsem, frsem).wait_send()
    loop(0, rhalf, relay)

    after_first(g2r, a2s, a2r).wait_recv()
    part3 = g2s[...]
    for d in range(1, nrow):
        part3 += g2r[d]
    gwo[0] = part3[0:wrows] * scale
    gb_out[...] = jnp.sum(part3[wrows:wrows + 8], axis=0, keepdims=True) * scale
    run(ncol, lambda d: a3(d).start())

    after_first(brecv, bsem, brsem).wait_recv()

    scan_loop(ncol, 19, lambda j: brecv[meta_s[16, j]].astype(F32))

    per = width // blk

    def gf_copy(p):
        s = pl.ds(pl.multiple_of(p * width, width), width)
        return pltpu.make_async_copy(gfv.at[s], gf_out.at[s], lsem.at[13 + p])

    def prepare(p, direct, from_side):
        total = summed(0, p)
        direct(p).wait_recv()
        pa[0, p] = total + rb[from_side, p].astype(F32)

    def finish(p, relayed, from_side):
        relayed(p).wait_recv()
        total = pa[0, p] + rb[from_side, p].astype(F32)
        for h in range(per):
            k = p * per + h
            block = total[:, h * blk:(h + 1) * blk] + scan[meta_s[18, k]]
            gfv[pl.ds(pl.multiple_of(k * blk, blk), blk), :] = block.T.astype(BF16)
        gf_copy(p).start()

    for i in range(rhalf):
        prepare(i, last_left, 0)
        prepare(RS - 1 - i, last_right, 1)
    after_first(bst, bsem, brsem).wait_send()
    after_first(gwr, a1s, a1r).wait_send()
    after_first(g2r, a2s, a2r).wait_send()
    for i in range(rhalf):
        finish(i, last_right, 1)
        finish(RS - 1 - i, last_left, 0)

    after_first(gwo, a3s, a3r).wait_recv()

    def place(d):
        at = pl.multiple_of(back_peer(d) * wrows, wrows)
        gw_out[pl.ds(at, wrows), :] = gwo[d]

    loop(0, ncol, place)
    after_first(gwo, a3s, a3r).wait_send()
    whole(fg, tsem, tsem).wait_send()
    hid_copy.wait()
    loop(0, RS, lambda p: gf_copy(p).wait())


def hand_over(*refs):
    sems = refs[-1]
    copies = [pltpu.make_async_copy(refs[i], refs[4 + i], sems.at[i]) for i in range(4)]
    for copy in copies:
        copy.start()
    for copy in copies:
        copy.wait()


def solution(mesh):
    nrow, ncol = mesh.shape["row"], mesh.shape["col"]

    def body(features, weight, bias_vector, stripe_values, tile_values, tile_rows, tile_slots, send_lists, cotangent):
        nodes, f = features.shape
        nt, blk, _ = tile_values.shape
        nblk = nodes // blk
        wrows = blk // ncol
        scale = 1.0 / math.sqrt(nodes * nrow * ncol)
        vm = pltpu.VMEM
        dma = pltpu.SemaphoreType.DMA
        copies = 6 * AG + 1 + 7 * RS
        any_, vmem, smem = (pl.BlockSpec(memory_space=m) for m in (pl.ANY, pltpu.VMEM, pltpu.SMEM))
        shapes = (
            jax.ShapeDtypeStruct((nodes, f), BF16),
            jax.ShapeDtypeStruct((nodes, f), BF16),
            jax.ShapeDtypeStruct((f, f), F32),
            jax.ShapeDtypeStruct((1, f), F32),
        )
        made = pl.pallas_call(
            functools.partial(kernel, nrow, ncol, scale),
            out_shape=shapes,
            in_specs=[any_] * 9,
            out_specs=(any_, any_, vmem, vmem),
            scratch_shapes=[
                vm((f, f), BF16),
                vm((1, f), F32),
                pltpu.SMEM((nt,), jnp.int32),
                pltpu.SMEM((nt,), jnp.int32),
                pltpu.SMEM((ncol,), jnp.int32),
                vm((8, nodes, nodes), BF16),
                vm((nblk, blk, f), BF16),
                vm((7, nblk, blk, f), BF16),
                vm((nt, blk, blk), BF16),
                vm((nodes, f), BF16),
                vm((ncol, blk, f), BF16),
                vm((ncol, blk, f), BF16),
                vm((24, 128), jnp.int32),
                pltpu.SMEM((24, 128), jnp.int32),
                vm((nt + 1, blk, blk), F32),
                vm((nodes, f), F32),
                vm((nodes, f), BF16),
                vm((nodes, f), BF16),
                vm((nodes, f), BF16),
                vm((f, nodes), BF16),
                vm((nblk, f, blk), BF16),
                vm((4, RS, f, nodes // RS), F32),
                vm((4, RS, f, nodes // RS), BF16),
                vm((4, RS, f, nodes // RS), BF16),
                vm((3, RS, f, nodes // RS), BF16),
                vm((RS, f, nodes // RS), BF16),
                vm((2, RS, f, nodes // RS), BF16),
                vm((ncol, f, blk), BF16),
                vm((ncol, f, blk), BF16),
                vm((ncol, wrows + 8, f), F32),
                vm((ncol, wrows + 8, f), F32),
                vm((wrows + 8, f), F32),
                vm((nrow, wrows + 8, f), F32),
                vm((ncol, wrows, f), F32),
                vm((nodes, f), BF16),
                vm((8, f), F32),
                dma((18 + RS,)),
                dma((copies,)),
                dma(()), dma(()), dma(()), dma(()), dma(()), dma(()),
                pltpu.SemaphoreType.REGULAR,
                dma(()), dma(()), dma(()), dma(()), dma(()), dma(()),
            ],
            compiler_params=pltpu.CompilerParams(
                collective_id=0, has_side_effects=True, vmem_limit_bytes=56 * 2**20
            ),
        )(
            features.reshape(nblk, blk, f), weight, bias_vector.reshape(1, f), stripe_values, tile_values,
            tile_rows, tile_slots, send_lists.reshape(ncol), cotangent,
        )
        hid, gf, gw, gb = pl.pallas_call(
            hand_over, out_shape=shapes, in_specs=[vmem] * 4, out_specs=(any_,) * 4, scratch_shapes=[dma((4,))]
        )(*made)
        return hid, gf, gw, gb.reshape(f)

    return jax.shard_map(
        body,
        mesh=mesh,
        in_specs=(
            P(("row", "col"), None),
            P(),
            P(),
            P(("row", "col"), None),
            P(("row", "col"), None, None),
            P(("row", "col")),
            P(("row", "col")),
            P("row", "col", None, None),
            P(("row", "col"), None),
        ),
        out_specs=(P(("row", "col"), None), P(("row", "col"), None), P(), P()),
        check_vma=False,
    )
```

```python
import functools
import math

import jax
import jax.numpy as jnp
from jax import lax
from jax.experimental import pallas as pl
from jax.experimental.pallas import tpu as pltpu
from jax.sharding import PartitionSpec as P

MESH = pl.DeviceIdType.MESH
BF16 = jnp.bfloat16
F32 = jnp.float32
AG = 2
RS = 2


def mm(a, b):
    return jnp.dot(a, b, preferred_element_type=F32)


def order(read, n, lanes=128):
    sub = lax.broadcasted_iota(jnp.int32, (n, lanes), 0)
    lane = lax.broadcasted_iota(jnp.int32, (n, lanes), 1)
    col = jnp.zeros((n, lanes), jnp.int32)
    row = jnp.full((n, lanes), 1 << 20, jnp.int32)

    def one(t, both):
        v = read(t)
        return jnp.where(sub == t, v, both[0]), jnp.where(lane == t, v * n + t, both[1])

    col, row = lax.fori_loop(0, n, one, (col, row))
    less = (row < col * n + sub).astype(jnp.int32)
    rank = jnp.sum(less, axis=1, keepdims=True)
    hit = rank == lane
    perm = jnp.sum(jnp.where(hit, sub, 0), axis=0, keepdims=True)
    value = jnp.sum(jnp.where(hit, col, 0), axis=0, keepdims=True)
    last = jnp.sum((col <= lane).astype(jnp.int32), axis=0, keepdims=True)
    count = jnp.sum((col == lane).astype(jnp.int32), axis=0, keepdims=True)
    last = jnp.where(count > 0, last, 0)
    before = jnp.sum(((row // n == col) & (lane < sub)).astype(jnp.int32), axis=1, keepdims=True)
    again = jnp.sum(jnp.where(hit & (before > 0), 1, 0), axis=0, keepdims=True)
    return jnp.concatenate([perm, value, last, again] + [jnp.zeros_like(perm)] * 4, axis=0)


def kernel(
    nrow, ncol, scale,
    feat, weight_h, bias_h, stripe, tiles, rows_h, slots_h, lists_h, cot,
    hid_out, gf_out, gw_out, gb_out,
    weight, bias, rows_s, slots_s, lists_s, st, fo, fg, tv, cv, recv, stage, meta_v, meta_s, scan, y, yb, gp, hid, gt, gtb,
    pa, ps, sr, xs, ra, rb, bst, brecv, gws, gwr, g2s, g2r, gwo, gfv, biasp,
    lsem, rsem, fsem, frsem, bsem, brsem, gsem, tsem, heard, a1s, a1r, a2s, a2r, a3s, a3r,
):
    nblk, blk, _ = feat.shape
    nt = tv.shape[0]
    nodes = nblk * blk
    small = [
        pltpu.make_async_copy(x, y_, lsem.at[13 + RS + i])
        for i, (x, y_) in enumerate(
            [(rows_h, rows_s), (slots_h, slots_s), (lists_h, lists_s), (weight_h, weight), (bias_h, bias)]
        )
    ]
    r = lax.axis_index("row")
    c = lax.axis_index("col")
    chip, core = r // 2, r % 2
    chips = nrow // 2
    chip_r, chip_l, chip_f = (chip + 1) % chips, (chip + chips - 1) % chips, (chip + 2) % chips
    sib = chip * 2 + 1 - core
    right, left = chip_r * 2 + core, chip_l * 2 + core
    order_of = [
        chip * 2 + core, chip * 2 + 1 - core,
        chip_l * 2 + core, chip_l * 2 + 1 - core,
        chip_r * 2 + core, chip_r * 2 + 1 - core,
        chip_f * 2 + core, chip_f * 2 + 1 - core,
    ]

    side = next(k for k in range(1, ncol + 1) if k * k >= ncol)
    lines = ncol // side
    cy, cz = c // side, c % side

    def peer(d):
        return lax.rem(cy + d // side, lines) * side + lax.rem(cz + d % side, side)

    def back_peer(d):
        return lax.rem(cy + lines - d // side, lines) * side + lax.rem(cz + side - d % side, side)

    def offset(q):
        return lax.rem(cy + lines - q // side, lines) * side + lax.rem(cz + side - q % side, side)

    local = [
        pltpu.make_async_copy(feat, fo, lsem.at[8]),
        pltpu.make_async_copy(cot, cv, lsem.at[9]),
        pltpu.make_async_copy(tiles, tv, lsem.at[10]),
    ]
    barrier = pltpu.get_barrier_semaphore()

    others = [(row, c) for row in (sib, right, left)]
    z_peers = [(r, cy * side + (cz + d) % side) for d in range(1, side)]
    y_peers = [(r, (cy + d) % lines * side + cz) for d in range(1, lines)]
    for dev in others + z_peers + y_peers:
        pl.semaphore_signal(barrier, inc=1, device_id=dev, device_id_type=MESH)

    for copy in small:
        copy.start()
    local[0].start()
    stripes = [
        pltpu.make_async_copy(
            stripe.at[:, pl.ds(pl.multiple_of(order_of[k] * nodes, 128), nodes)], st.at[k], lsem.at[k]
        )
        for k in range(8)
    ]
    stripes[0].start()
    stripes[1].start()
    for k in range(2, 8):
        stripes[k].start()
    local[2].start()
    local[1].start()
    for copy in small:
        copy.wait()
    meta_v[0:8] = order(lambda t: rows_s[t], nt)
    meta_v[8:16] = order(lambda t: offset(slots_s[t]), nt)
    meta_v[16:24] = order(lambda d: lists_s[peer(d)], ncol)
    meta_copy = pltpu.make_async_copy(meta_v, meta_s, lsem.at[11])
    meta_copy.start()

    pl.semaphore_wait(barrier, len(others + z_peers + y_peers))
    for dev in z_peers:
        pl.semaphore_signal(heard, inc=1, device_id=dev, device_id_type=MESH)

    piece, half = nodes // AG, AG // 2
    pb = piece // blk
    width, rhalf = nodes // RS, RS // 2

    def remote(i, src, dst, row, sent=gsem):
        return pltpu.make_async_remote_copy(
            src_ref=src, dst_ref=dst, send_sem=sent, recv_sem=rsem.at[i],
            device_id=(row, c), device_id_type=MESH,
        )

    def whole(ref, sent, received):
        return pltpu.make_async_remote_copy(
            src_ref=ref, dst_ref=ref, send_sem=sent, recv_sem=received,
            device_id=(sib, c), device_id_type=MESH,
        )

    def after_first(ref, sent, received):
        return whole(ref.at[pl.ds(1, ref.shape[0] - 1)], sent, received)

    def part(slot, p):
        own = fo if slot == 0 else fg.at[slot - 1]
        return own.at[pl.ds(p * pb, pb)]

    def own_right(p):
        return remote(p, part(0, p), part(2, p), right)

    def own_left(p):
        return remote(AG + p, part(0, p), part(4, p), left)

    def on_right(p):
        return remote(2 * AG + p, part(2, p), part(6, p), right)

    def on_left(p):
        return remote(2 * AG + p, part(4, p), part(6, p), left)

    def to_twin(slot, p):
        return remote(3 * AG + (slot - 2) // 2 * AG + p, part(slot, p), part(slot + 1, p), sib)

    own_twin = remote(6 * AG, fo, fg.at[0], sib)
    base = 6 * AG + 1

    def give(q, p):
        return remote(base + q * RS + p, ps.at[q, p], sr.at[q, p], sib, tsem)

    def first_right(p):
        return remote(base + 4 * RS + p, xs.at[2, p], ra.at[p], right, tsem)

    def first_left(p):
        return remote(base + 4 * RS + p, xs.at[2, p], ra.at[p], left, tsem)

    def last_right(p):
        return remote(base + 5 * RS + p, xs.at[1, p], rb.at[1, p], right, tsem)

    def last_left(p):
        return remote(base + 6 * RS + p, xs.at[0, p], rb.at[0, p], left, tsem)

    def loop(start, stop, act):
        def one(d, _):
            act(d)
            return 0

        lax.fori_loop(start, stop, one, 0)

    local[0].wait()
    own_right(0).start()
    own_left(AG - 1).start()
    own_twin.start()

    def own(i):
        own_right(i).start()
        own_left(AG - 1 - i).start()

    loop(1, AG, own)
    def block_copy(d):
        return pltpu.make_async_remote_copy(
            src_ref=stage.at[d], dst_ref=recv.at[d], send_sem=fsem, recv_sem=frsem,
            device_id=(r, peer(d)), device_id_type=MESH,
        )

    def picked(d):
        return fo[lists_s[peer(d)]]

    def send_block(d):
        stage[d] = picked(d)
        block_copy(d).start()

    def send_blocks():
        pl.semaphore_wait(heard, len(z_peers))
        for i in range(1, lines):
            loop(i * side + 1, (i + 1) * side, send_block)

    loop(1, side, send_block)
    loop(1, lines, lambda i: send_block(i * side))
    recv[0] = picked(0)

    def dense_all(slot, fresh):
        rows = nodes // 2
        src = fo if slot == 0 else fg.at[slot - 1]

        def one(i):
            at = pl.ds(pl.multiple_of(i * rows, rows), rows)
            v = mm(st[slot, at, :], src[...].reshape(nodes, -1))
            y[at, :] = v if fresh else y[at, :] + v

        loop(0, 2, one)

    stripes[0].wait()
    dense_all(0, True)
    stripes[1].wait()
    own_twin.wait_recv()
    dense_all(1, False)
    scan[0] = jnp.zeros((blk, blk), F32)

    def same(row, j):
        return meta_s[row, j].astype(F32)

    unroll = 16

    def scan_loop(n, row, term):
        def step(i):
            terms = [term(i * unroll + u) for u in range(unroll)]
            run_sum = scan[i * unroll]
            for u in range(unroll):
                run_sum = terms[u] + same(row, i * unroll + u) * run_sum
                scan[i * unroll + u + 1] = run_sum

        loop(0, n // unroll, step)

    def sparse_forward():
        meta_copy.wait()
        local[2].wait()
        after_first(recv, fsem, frsem).wait_recv()

        def product(j):
            t = meta_s[0, j]
            return mm(tv[t], recv[offset(slots_s[t])])

        scan_loop(nt, 3, product)

        def put(k):
            y[pl.ds(pl.multiple_of(k * blk, blk), blk), :] += scan[meta_s[2, k]]

        loop(0, nblk, put)

    def add(one, p, two, q):
        rows = nodes // 2

        def half_rows(i):
            at = pl.ds(pl.multiple_of(i * rows, rows), rows)
            parts = [
                mm(st[slot, at, u * piece:(u + 1) * piece], fg[slot - 1, u * pb:(u + 1) * pb].reshape(piece, -1))
                for slot, u in ((one, p), (two, q))
            ]
            y[at, :] += parts[0] + parts[1]

        loop(0, 2, half_rows)

    def arrive(i):
        j = AG - 1 - i
        own_right(i).wait_recv()
        if i < half:
            on_right(i).start()
        to_twin(2, i).start()
        own_left(j).wait_recv()
        if i < half:
            on_left(j).start()
        to_twin(4, j).start()

    def twins(i):
        j = AG - 1 - i
        to_twin(2, i).wait_recv()
        to_twin(4, j).wait_recv()
        add(3, i, 5, j)

    def arrive_far(i):
        j = AG - 1 - i
        on_right(i).wait_recv()
        to_twin(6, i).start()
        on_left(j).wait_recv()
        to_twin(6, j).start()

    def far_twins(i):
        j = AG - 1 - i
        to_twin(6, i).wait_recv()
        to_twin(6, j).wait_recv()
        add(7, i, 7, j)

    send_blocks()
    for i in range(AG):
        arrive(i)
        if i == 0:
            stripes[2].wait()
            stripes[4].wait()
        add(2, i, 4, AG - 1 - i)
        if i == 0:
            stripes[3].wait()
            stripes[5].wait()
        else:
            twins(i - 1)
    twins(AG - 1)
    stripes[6].wait()
    stripes[7].wait()
    for i in range(half):
        arrive_far(i)
        add(6, i, 6, AG - 1 - i)
        if i == 0:
            sparse_forward()
        else:
            far_twins(i - 1)
    far_twins(half - 1)

    local[1].wait()
    w = weight[...]
    chunk = 8 * blk
    biasp[...] = jnp.zeros_like(biasp)

    def pointwise(k):
        s = pl.ds(pl.multiple_of(k * chunk, chunk), chunk)
        yk = y[s, :].astype(BF16)
        yb[s, :] = yk
        x = mm(yk, w) + bias[...]
        g = jax.nn.sigmoid(x)
        hid[s, :] = (x * g).astype(BF16)
        gk = (cv[s, :].astype(F32) * (g * (1.0 + x * (1.0 - g)))).astype(BF16)
        gp[s, :] = gk
        biasp[...] += jnp.sum(gk.astype(F32).reshape(chunk // 8, 8, blk), axis=0)
        gtk = lax.dot_general(w, gk, (((1,), (1,)), ((), ())), preferred_element_type=F32).astype(BF16)
        gt[:, s] = gtk
        for h in range(8):
            gtb[8 * k + h] = gtk[:, h * blk:(h + 1) * blk]

    loop(0, nodes // chunk, pointwise)
    hid_copy = pltpu.make_async_copy(hid, hid_out, lsem.at[12])
    hid_copy.start()

    group = min(2, RS)

    def back(slot, i):
        wide = group * width
        return mm(gt[...], st[slot, :, pl.ds(pl.multiple_of(i * wide, wide), wide)])

    def send_sib(q):
        def one(i):
            v = back(2 * q + 1, i).astype(BF16)
            for u in range(group):
                ps[q, i * group + u] = v[:, u * width:(u + 1) * width]
                give(q, i * group + u).start()

        loop(0, RS // group, one)

    def keep_own(q):
        def one(i):
            v = back(2 * q, i)
            for u in range(group):
                pa[q, i * group + u] = v[:, u * width:(u + 1) * width]

        loop(0, RS // group, one)

    def summed(q, p):
        give(q, p).wait_recv()
        return pa[q, p] + sr[q, p].astype(F32)

    send_sib(3)

    gw = lax.dot_general(yb[...], gp[...], (((0,), (0,)), ((), ())), preferred_element_type=F32)
    wrows = blk // ncol
    for q in range(ncol):
        gws[q, 0:wrows] = gw[q * wrows:(q + 1) * wrows, :]
        gws[q, wrows:wrows + 8] = biasp[...]

    def a1(d):
        return pltpu.make_async_remote_copy(
            src_ref=gws.at[peer(d)], dst_ref=gwr.at[d], send_sem=a1s, recv_sem=a1r,
            device_id=(r, peer(d)), device_id_type=MESH,
        )

    def a2(d):
        return pltpu.make_async_remote_copy(
            src_ref=g2s, dst_ref=g2r.at[d], send_sem=a2s, recv_sem=a2r,
            device_id=(lax.rem(r + d, nrow), c), device_id_type=MESH,
        )

    def a3(d):
        return pltpu.make_async_remote_copy(
            src_ref=gwo.at[0], dst_ref=gwo.at[d], send_sem=a3s, recv_sem=a3r,
            device_id=(r, peer(d)), device_id_type=MESH,
        )

    def run(n, act):
        loop(1, n, act)

    run(ncol, lambda d: a1(d).start())

    keep_own(3)

    def first(i):
        j = RS - 1 - i
        xs[2, i] = summed(3, i).astype(BF16)
        first_right(i).start()
        xs[2, j] = summed(3, j).astype(BF16)
        first_left(j).start()

    loop(0, rhalf, first)

    def back_copy(d):
        return pltpu.make_async_remote_copy(
            src_ref=bst.at[d], dst_ref=brecv.at[d], send_sem=bsem, recv_sem=brsem,
            device_id=(r, back_peer(d)), device_id_type=MESH,
        )

    def bproduct(j):
        t = meta_s[8, j]
        return mm(gtb[rows_s[t]], tv[t])

    scan_loop(nt, 11, bproduct)

    def slot_sum(d):
        return scan[meta_s[10, d]].astype(BF16)

    brecv[0] = slot_sum(0)

    def send_back(d, _):
        bst[d] = slot_sum(d)
        back_copy(d).start()
        return 0

    lax.fori_loop(1, ncol, send_back, 0)

    send_sib(2)
    send_sib(1)
    keep_own(2)
    keep_own(1)
    after_first(gwr, a1s, a1r).wait_recv()
    part2 = gws[c]
    for d in range(1, ncol):
        part2 += gwr[d]
    g2s[...] = part2
    run(nrow, lambda d: a2(d).start())


    def direct(i):
        j = RS - 1 - i
        xs[1, j] = summed(2, j).astype(BF16)
        last_right(j).start()
        xs[0, i] = summed(1, i).astype(BF16)
        last_left(i).start()

    loop(0, rhalf, direct)
    send_sib(0)
    keep_own(0)

    def relay(i):
        j = RS - 1 - i
        first_right(i).wait_recv()
        xs[1, i] = (summed(2, i) + ra[i].astype(F32)).astype(BF16)
        last_right(i).start()
        first_left(j).wait_recv()
        xs[0, j] = (summed(1, j) + ra[j].astype(F32)).astype(BF16)
        last_left(j).start()

    whole(fg, gsem, gsem).wait_send()
    after_first(stage, fsem, frsem).wait_send()
    loop(0, rhalf, relay)

    after_first(g2r, a2s, a2r).wait_recv()
    part3 = g2s[...]
    for d in range(1, nrow):
        part3 += g2r[d]
    gwo[0] = part3[0:wrows] * scale
    gb_out[...] = jnp.sum(part3[wrows:wrows + 8], axis=0, keepdims=True) * scale
    run(ncol, lambda d: a3(d).start())

    after_first(brecv, bsem, brsem).wait_recv()

    scan_loop(ncol, 19, lambda j: brecv[meta_s[16, j]].astype(F32))

    per = width // blk

    def gf_copy(p):
        s = pl.ds(pl.multiple_of(p * width, width), width)
        return pltpu.make_async_copy(gfv.at[s], gf_out.at[s], lsem.at[13 + p])

    def prepare(p, direct, from_side):
        total = summed(0, p)
        direct(p).wait_recv()
        pa[0, p] = total + rb[from_side, p].astype(F32)

    def finish(p, relayed, from_side):
        relayed(p).wait_recv()
        total = pa[0, p] + rb[from_side, p].astype(F32)
        for h in range(per):
            k = p * per + h
            block = total[:, h * blk:(h + 1) * blk] + scan[meta_s[18, k]]
            gfv[pl.ds(pl.multiple_of(k * blk, blk), blk), :] = block.T.astype(BF16)
        gf_copy(p).start()

    for i in range(rhalf):
        prepare(i, last_left, 0)
        prepare(RS - 1 - i, last_right, 1)
    after_first(bst, bsem, brsem).wait_send()
    after_first(gwr, a1s, a1r).wait_send()
    after_first(g2r, a2s, a2r).wait_send()
    for i in range(rhalf):
        finish(i, last_right, 1)
        finish(RS - 1 - i, last_left, 0)

    after_first(gwo, a3s, a3r).wait_recv()

    def place(d):
        at = pl.multiple_of(back_peer(d) * wrows, wrows)
        gw_out[pl.ds(at, wrows), :] = gwo[d]

    loop(0, ncol, place)
    after_first(gwo, a3s, a3r).wait_send()
    whole(fg, tsem, tsem).wait_send()
    hid_copy.wait()
    loop(0, RS, lambda p: gf_copy(p).wait())


def hand_over(*refs):
    sems = refs[-1]
    copies = [pltpu.make_async_copy(refs[i], refs[4 + i], sems.at[i]) for i in range(4)]
    for copy in copies:
        copy.start()
    for copy in copies:
        copy.wait()


def solution(mesh):
    nrow, ncol = mesh.shape["row"], mesh.shape["col"]

    def body(features, weight, bias_vector, stripe_values, tile_values, tile_rows, tile_slots, send_lists, cotangent):
        nodes, f = features.shape
        nt, blk, _ = tile_values.shape
        nblk = nodes // blk
        wrows = blk // ncol
        scale = 1.0 / math.sqrt(nodes * nrow * ncol)
        vm = pltpu.VMEM
        dma = pltpu.SemaphoreType.DMA
        copies = 6 * AG + 1 + 7 * RS
        any_, vmem, smem = (pl.BlockSpec(memory_space=m) for m in (pl.ANY, pltpu.VMEM, pltpu.SMEM))
        shapes = (
            jax.ShapeDtypeStruct((nodes, f), BF16),
            jax.ShapeDtypeStruct((nodes, f), BF16),
            jax.ShapeDtypeStruct((f, f), F32),
            jax.ShapeDtypeStruct((1, f), F32),
        )
        made = pl.pallas_call(
            functools.partial(kernel, nrow, ncol, scale),
            out_shape=shapes,
            in_specs=[any_] * 9,
            out_specs=(any_, any_, vmem, vmem),
            scratch_shapes=[
                vm((f, f), BF16),
                vm((1, f), F32),
                pltpu.SMEM((nt,), jnp.int32),
                pltpu.SMEM((nt,), jnp.int32),
                pltpu.SMEM((ncol,), jnp.int32),
                vm((8, nodes, nodes), BF16),
                vm((nblk, blk, f), BF16),
                vm((7, nblk, blk, f), BF16),
                vm((nt, blk, blk), BF16),
                vm((nodes, f), BF16),
                vm((ncol, blk, f), BF16),
                vm((ncol, blk, f), BF16),
                vm((24, 128), jnp.int32),
                pltpu.SMEM((24, 128), jnp.int32),
                vm((nt + 1, blk, blk), F32),
                vm((nodes, f), F32),
                vm((nodes, f), BF16),
                vm((nodes, f), BF16),
                vm((nodes, f), BF16),
                vm((f, nodes), BF16),
                vm((nblk, f, blk), BF16),
                vm((4, RS, f, nodes // RS), F32),
                vm((4, RS, f, nodes // RS), BF16),
                vm((4, RS, f, nodes // RS), BF16),
                vm((3, RS, f, nodes // RS), BF16),
                vm((RS, f, nodes // RS), BF16),
                vm((2, RS, f, nodes // RS), BF16),
                vm((ncol, f, blk), BF16),
                vm((ncol, f, blk), BF16),
                vm((ncol, wrows + 8, f), F32),
                vm((ncol, wrows + 8, f), F32),
                vm((wrows + 8, f), F32),
                vm((nrow, wrows + 8, f), F32),
                vm((ncol, wrows, f), F32),
                vm((nodes, f), BF16),
                vm((8, f), F32),
                dma((18 + RS,)),
                dma((copies,)),
                dma(()), dma(()), dma(()), dma(()), dma(()), dma(()),
                pltpu.SemaphoreType.REGULAR,
                dma(()), dma(()), dma(()), dma(()), dma(()), dma(()),
            ],
            compiler_params=pltpu.CompilerParams(
                collective_id=0, has_side_effects=True, vmem_limit_bytes=56 * 2**20
            ),
        )(
            features.reshape(nblk, blk, f), weight, bias_vector.reshape(1, f), stripe_values, tile_values,
            tile_rows, tile_slots, send_lists.reshape(ncol), cotangent,
        )
        hid, gf, gw, gb = pl.pallas_call(
            hand_over, out_shape=shapes, in_specs=[vmem] * 4, out_specs=(any_,) * 4, scratch_shapes=[dma((4,))]
        )(*made)
        return hid, gf, gw, gb.reshape(f)

    return jax.shard_map(
        body,
        mesh=mesh,
        in_specs=(
            P(("row", "col"), None),
            P(),
            P(),
            P(("row", "col"), None),
            P(("row", "col"), None, None),
            P(("row", "col")),
            P(("row", "col")),
            P("row", "col", None, None),
            P(("row", "col"), None),
        ),
        out_specs=(P(("row", "col"), None), P(("row", "col"), None), P(), P()),
        check_vma=False,
    )
```
